256 devices in a mesh: tm: 16 (over z, core), tile: 16 (over y, x).
Axes of the slice: x: 4, y: 4, z: 8, core: 2. Of those that a mesh axis runs over, the one named last changes fastest.
Arguments:
- video: bfloat16 [512, 2, 8, 256, 128], P('tm', None, None, 'tile')
- slot_block: int32 [512], P('tm'), may hold values from -1 to 255, as said below
- clip_frames: int32 [8], replicated, may hold values from 1 to 128, 512 in all
- conv1_weight: bfloat16 [3, 3, 3, 128, 128], replicated, may hold values from -0.109375 to 0.109375
- norm_gain: float32 [128], replicated, may hold values from 0.5 to 1.5
- norm_bias: float32 [128], replicated, may hold values from -3 to 3
- conv2_weight: bfloat16 [3, 3, 3, 128, 128], replicated, may hold values from -0.109375 to 0.109375
- conv2_bias: float32 [128], replicated, may hold values from -3 to 3
Outputs:
- encoded: bfloat16 [512, 8, 256, 128], P('tm', None, 'tile')
The draws below stay inside these ranges and needn't reach their ends.
Inputs may be any that keep to these rules, and one draw needn't show every extreme that they name: `slot_block`: each of the 256 blocks of the pack sits in exactly one slot and the other slots hold -1; block k belongs to owner k // 16, and the slots of one index of tm hold at most 2 blocks of any one owner. `clip_frames`: the counts sum to 512.
All inputs are finite; a program needn't handle non-finite values.
Results may differ from the reference program's by a relative error of at most 0.002.
Values may be sent and summed in bfloat16 or wider, within the bound.
No kernel may reach another device: no remote copies, remote signals or barrier semaphores. Data moves between devices by JAX's collectives and lax.ppermute only.
A program may use at most 128 MiB of HBM per device.

```python
import math
import jax
import jax.numpy as jnp
import numpy as np
from jax import lax

C = 128
GROUPS = 32
ROWS = 8
CF = 2
OWN = 16
CLIPS = 8
SLOTS = 32
W = 256
FRAMES = 512
MOST = 128
N_TM = 16


def draw_video(key, part):
    key = jax.random.fold_in(key, 11)
    key_values, key_scale = jax.random.split(key, 2)
    full_shape = (N_TM * SLOTS, CF, ROWS, W, C)
    column = jnp.arange(W, dtype=jnp.float32) / (W - 1)
    column_trend = jnp.exp(column * math.log(3.0))[None, None, None, :, None]
    pixel_scale = jnp.exp(jax.random.uniform(key_scale, full_shape[:4] + (1,), jnp.float32) * math.log(10.0))
    values = jax.random.truncated_normal(key_values, -4.0, 4.0, full_shape, jnp.float32)
    return (values * column_trend * pixel_scale / 4.0).astype(jnp.bfloat16)


def shuffle_row(key_row):
    return jax.random.permutation(key_row, SLOTS)


def draw_slot_block(key, part):
    key = jax.random.fold_in(key, 23)
    key_surplus, key_order, key_slots = jax.random.split(key, 3)
    paired = N_TM // 2
    surplus = jax.random.randint(key_surplus, (paired,), 0, SLOTS - OWN + 1).astype(jnp.int32)
    surplus = surplus.at[0].set(SLOTS - OWN)
    deltas = jnp.concatenate([surplus, -surplus])
    held_counts = OWN + jax.random.permutation(key_order, deltas)
    before = jnp.cumsum(held_counts) - held_counts
    slot_ids = jnp.arange(SLOTS, dtype=jnp.int32)
    unit_ids = before[:, None] + slot_ids[None, :]
    owner_ids = unit_ids % N_TM
    block_ids = owner_ids * OWN + unit_ids // N_TM
    filled = jnp.where(slot_ids[None, :] < held_counts[:, None], block_ids, -1)
    orders = jax.vmap(shuffle_row)(jax.random.split(key_slots, N_TM))
    shuffled = jnp.take_along_axis(filled, orders, axis=1)
    return shuffled.reshape(N_TM * SLOTS).astype(jnp.int32)


def split_up(count, total, bound, slope):
    weights = [(1 << 20) // math.isqrt(rank ** slope) + 1 for rank in range(2, count + 1)]
    rest, given = total - bound - (count - 1), [1] * (count - 1)
    while rest > 0:
        free = [i for i in range(count - 1) if given[i] < bound]
        whole, budget = sum([weights[i] for i in free]), rest
        for i in free:
            more = min(bound - given[i], max(1, budget * weights[i] // whole), rest)
            given[i] = given[i] + more
            rest = rest - more
    return np.array([bound] + given)


def ragged(stream_key, number_of, total, limit, lean):
    if number_of == 2:
        one = jax.random.randint(stream_key, (), max(1, total - limit), min(limit, total - 1) + 1)
        return jnp.stack([one, total - one])
    sizes = jnp.asarray(split_up(number_of, total, limit, lean), jnp.int32)
    twos = (number_of - 1) // 2
    source_of, receiver = sizes[1:1 + 2 * twos:2], sizes[2:2 + 2 * twos:2]
    room = jnp.minimum(source_of - 1, limit - receiver)
    passed = jax.random.randint(jax.random.fold_in(stream_key, 1), (twos,), 0, 1 << 20) % (room + 1)
    sizes = sizes.at[1:1 + 2 * twos:2].set(source_of - passed).at[2:2 + 2 * twos:2].set(receiver + passed)
    return sizes[jax.random.permutation(jax.random.fold_in(stream_key, 2), number_of)]


def bell_draw(key, shape, scale, limit, held_as=jnp.bfloat16):
    entries = scale * jax.random.normal(key, shape, jnp.float32)
    return jnp.clip(entries, min=-limit, max=limit).astype(held_as)


def setup_inputs(seed: int = 0) -> dict:
    keys = jax.random.split(jax.random.key(seed), 9)
    video = draw_video(jax.random.fold_in(keys[8], 71), 0)
    slot_block = draw_slot_block(jax.random.fold_in(keys[8], 71), 0)
    clip_frames = ragged(keys[2], CLIPS, FRAMES, MOST, 2).astype(jnp.int32)
    conv1_weight = bell_draw(keys[3], (3, 3, 3, C, C), (27 * C) ** -0.5, 0.109375)
    norm_gain = jnp.clip(jax.random.uniform(keys[4], (C,), jnp.float32, 0.5, 1.5), 0.5, 1.5)
    norm_bias = bell_draw(keys[5], (C,), 0.5, 3.0, jnp.float32)
    conv2_weight = bell_draw(keys[6], (3, 3, 3, C, C), (27 * C) ** -0.5, 0.109375)
    conv2_bias = bell_draw(keys[7], (C,), 0.5, 3.0, jnp.float32)
    return dict(video=video, slot_block=slot_block, clip_frames=clip_frames, conv1_weight=conv1_weight, norm_gain=norm_gain, norm_bias=norm_bias, conv2_weight=conv2_weight, conv2_bias=conv2_bias)


epsilon = 1e-06

def frame_clips(clip_frames, first_frame, frame_count):
    clip_ends = jnp.cumsum(clip_frames).astype(jnp.int32)
    frame_index = first_frame + jnp.arange(frame_count, dtype=jnp.int32)
    clip_ids = lax.optimization_barrier(jnp.sum((frame_index[:, None] >= clip_ends[None, :]).astype(jnp.int32), axis=1))
    return jnp.where(frame_index < 0, -1, clip_ids).astype(jnp.int32)

def causal_conv(padded, clip_ids, weight):
    outputs = padded.shape[0] - 2
    height = padded.shape[1] - 2
    width = padded.shape[2] - 2
    channels = padded.shape[3]
    summed = jnp.zeros((outputs * height * width, weight.shape[4]), jnp.float32)
    for offset in range(3):
        valid_lag = (clip_ids[2 - offset:2 - offset + outputs] == clip_ids[2:]).astype(padded.dtype)
        source = padded[2 - offset:2 - offset + outputs] * valid_lag[:, None, None, None]
        windows = [source[:, row_tap:row_tap + height, col_tap:col_tap + width, :] for row_tap in range(3) for col_tap in range(3)]
        stacked = jnp.concatenate(windows, axis=3).reshape(outputs * height * width, 9 * channels)
        kernel = weight[2 - offset].reshape(9 * channels, weight.shape[4])
        summed = summed + jnp.dot(stacked, kernel, preferred_element_type=jnp.float32)
    return summed.reshape(outputs, height, width, weight.shape[4])

def group_norm_silu(hidden, norm_gain, norm_bias):
    frame_count, height, width, channels = hidden.shape
    grouped = hidden.reshape(frame_count, height, width, GROUPS, channels // GROUPS)
    group_mean = lax.optimization_barrier(jnp.mean(grouped, axis=(1, 2, 4), keepdims=True))
    centred = grouped - group_mean
    group_var = lax.optimization_barrier(jnp.mean(centred * centred, axis=(1, 2, 4), keepdims=True))
    normed = (centred * lax.rsqrt(group_var + epsilon)).reshape(hidden.shape)
    return jax.nn.silu(normed * norm_gain + norm_bias).astype(jnp.bfloat16)

def reference(video, slot_block, clip_frames, conv1_weight, norm_gain, norm_bias, conv2_weight, conv2_bias):
    blocks = N_TM * OWN
    target = jnp.where(slot_block < 0, blocks, slot_block).astype(jnp.int32)
    stream = jnp.zeros((blocks + 1,) + video.shape[1:], video.dtype).at[target].set(video)[:blocks]
    frames = stream.reshape(FRAMES, ROWS, W, C)
    clip_ids = frame_clips(clip_frames, -2, FRAMES + 2)
    frame_span = OWN * CF
    starts = jnp.arange(N_TM, dtype=jnp.int32) * frame_span
    padded = jnp.pad(frames, ((2, 0), (1, 1), (1, 1), (0, 0)))

    def first_layer(start):
        window_frames = lax.dynamic_slice_in_dim(padded, start, frame_span + 2, 0)
        window_clips = lax.dynamic_slice_in_dim(clip_ids, start, frame_span + 2, 0)
        hidden = causal_conv(window_frames, window_clips, conv1_weight)
        return group_norm_silu(hidden, norm_gain, norm_bias)
    active = lax.map(first_layer, starts).reshape(FRAMES, ROWS, W, C)
    padded_active = jnp.pad(active, ((2, 0), (1, 1), (1, 1), (0, 0)))

    def second_layer(start):
        window_frames = lax.dynamic_slice_in_dim(padded_active, start, frame_span + 2, 0)
        window_clips = lax.dynamic_slice_in_dim(clip_ids, start, frame_span + 2, 0)
        return causal_conv(window_frames, window_clips, conv2_weight)
    branch = lax.map(second_layer, starts).reshape(FRAMES, ROWS, W, C)
    return (frames.astype(jnp.float32) + branch + conv2_bias).astype(jnp.bfloat16)
```

```python
import functools

import jax
import jax.numpy as jnp
from jax import lax
from jax.experimental import pallas as pl
from jax.experimental.pallas import tpu as pltpu
from jax.sharding import PartitionSpec as P

GROUPS = 32
OWN = 16
CAP = 2
C = 128
ROWS = 8
COLS = 16
POS = ROWS * COLS
LEAD = 4
CHUNK = 4
EPSILON = 1e-06
VMEM_BYTES = 48 * 1024 * 1024

f32 = jnp.float32
bf16 = jnp.bfloat16


def vmem():
    return pl.BlockSpec(memory_space=pltpu.VMEM)


def smem():
    return pl.BlockSpec(memory_space=pltpu.SMEM)


def hbm():
    return pl.BlockSpec(memory_space=pl.ANY)


def params():
    return pltpu.CompilerParams(vmem_limit_bytes=VMEM_BYTES)


def send_kernel(slot_ref, video_ref, out_ref, count, sems):
    slots = slot_ref.shape[0]
    for owner in range(count.shape[0]):
        count[owner] = 0

    for slot in range(slots):
        block = slot_ref[slot]

        @pl.when(block >= 0)
        def _():
            owner = block >> 4
            rank = count[owner]
            count[owner] = rank + 1
            pltpu.make_async_copy(
                video_ref.at[slot], out_ref.at[owner * CAP + rank], sems.at[slot]
            ).start()

    for slot in range(slots):

        @pl.when(slot_ref[slot] >= 0)
        def _():
            pltpu.make_async_copy(video_ref.at[slot], out_ref.at[0], sems.at[slot]).wait()


def send_blocks(slot_block, video, owners):
    return pl.pallas_call(
        send_kernel,
        out_shape=jax.ShapeDtypeStruct((owners * CAP,) + video.shape[1:], video.dtype),
        in_specs=[smem(), hbm()],
        out_specs=hbm(),
        scratch_shapes=[
            pltpu.SMEM((owners,), jnp.int32),
            pltpu.SemaphoreType.DMA((video.shape[0],)),
        ],
        compiler_params=params(),
        name="send_blocks",
    )(slot_block, video)


def place_kernel(order_ref, arrived_ref, lead_ref, frames_ref, left_ref, right_ref, wide, sems):
    blocks = order_ref.shape[0]
    length = LEAD + blocks * 2
    copies = [
        pltpu.make_async_copy(
            arrived_ref.at[order_ref[k]],
            frames_ref.at[pl.ds(LEAD + 2 * k, 2)],
            sems.at[k],
        )
        for k in range(blocks)
    ]
    for copy in copies:
        copy.start()
    frames_ref[0:LEAD] = lead_ref[...]

    def edges(start):
        wide[...] = frames_ref[pl.ds(start, 2)].reshape(2 * POS, C).astype(f32)
        left = wide[pl.ds(0, 2 * ROWS, stride=COLS), :].astype(bf16)
        right = wide[pl.ds(COLS - 1, 2 * ROWS, stride=COLS), :].astype(bf16)
        left_ref[pl.ds(start, 2)] = left.reshape(2, ROWS, C)
        right_ref[pl.ds(start, 2)] = right.reshape(2, ROWS, C)

    for start in range(0, LEAD, 2):
        edges(start)
    for k in range(blocks):
        copies[k].wait()
        edges(LEAD + 2 * k)


def place_blocks(order, arrived, lead):
    blocks = order.shape[0]
    length = LEAD + 2 * blocks
    edge = jax.ShapeDtypeStruct((length, ROWS, C), bf16)
    return pl.pallas_call(
        place_kernel,
        out_shape=(jax.ShapeDtypeStruct((length, ROWS, COLS, C), bf16), edge, edge),
        in_specs=[smem(), hbm(), vmem()],
        out_specs=(vmem(), vmem(), vmem()),
        scratch_shapes=[
            pltpu.VMEM((2 * POS, C), f32),
            pltpu.SemaphoreType.DMA((blocks,)),
        ],
        compiler_params=params(),
        name="place_blocks",
    )(order, arrived, lead)


def conv_kernel(valid_ref, frames_ref, weight_ref, out_ref, shifted, taps):
    length = frames_ref.shape[0]
    rows = CHUNK * POS
    column = lax.broadcasted_iota(jnp.int32, (rows, C), 0) % COLS
    first = column == 0
    last = column == COLS - 1
    for j in range(3):
        taps[j, :, 0] = jnp.zeros((CHUNK, COLS, C), bf16)
        taps[j, :, ROWS + 1] = jnp.zeros((CHUNK, COLS, C), bf16)
    shifted[0:8] = jnp.zeros((8, C), f32)
    shifted[rows + 8 :] = jnp.zeros((8, C), f32)
    out_ref[0:2] = jnp.zeros((2, POS, C), f32)

    def step(chunk, carry):
        start = chunk * CHUNK
        here = frames_ref[pl.ds(start, CHUNK)]
        shifted[8 : rows + 8] = here.reshape(rows, C).astype(f32)
        before = jnp.where(first, 0.0, shifted[7 : rows + 7]).astype(bf16)
        after = jnp.where(last, 0.0, shifted[9 : rows + 9]).astype(bf16)
        taps[0, :, 1 : ROWS + 1] = before.reshape(CHUNK, ROWS, COLS, C)
        taps[1, :, 1 : ROWS + 1] = here
        taps[2, :, 1 : ROWS + 1] = after.reshape(CHUNK, ROWS, COLS, C)
        windows = jnp.concatenate(
            [taps[j, :, i : i + ROWS].reshape(rows, C) for j in range(3) for i in range(3)],
            axis=1,
        )
        product = jnp.dot(windows, weight_ref[...], preferred_element_type=f32)
        for q in range(CHUNK):
            frame = start + q
            part = product[q * POS : (q + 1) * POS]
            out_ref[frame] += part[:, 0:C]

            @pl.when(frame + 1 < length)
            def _():
                out_ref[frame + 1] += valid_ref[0, frame + 1] * part[:, C : 2 * C]

            @pl.when(frame + 2 < length)
            def _():
                out_ref[frame + 2] = valid_ref[1, frame + 2] * part[:, 2 * C :]

        return carry

    lax.fori_loop(0, length // CHUNK, step, 0)


def conv(valid, frames, weight):
    length = frames.shape[0]
    return pl.pallas_call(
        conv_kernel,
        out_shape=jax.ShapeDtypeStruct((length, POS, C), f32),
        in_specs=[smem(), vmem(), vmem()],
        out_specs=vmem(),
        scratch_shapes=[
            pltpu.VMEM((CHUNK * POS + 16, C), f32),
            pltpu.VMEM((3, CHUNK, ROWS + 2, COLS, C), bf16),
        ],
        compiler_params=params(),
        cost_estimate=pl.CostEstimate(
            flops=2 * length * POS * 27 * C * C, bytes_accessed=4 << 20, transcendentals=0
        ),
        name="conv",
    )(valid, frames, weight)


def edge_product(edge_ref, weight):
    length = edge_ref.shape[0]
    rows = length * ROWS
    edge = edge_ref[...].astype(f32).reshape(rows, C)
    row = lax.broadcasted_iota(jnp.int32, (rows, C), 0) % ROWS
    above = jnp.where(row == 0, 0.0, pltpu.roll(edge, 1, 0))
    below = jnp.where(row == ROWS - 1, 0.0, pltpu.roll(edge, rows - 1, 0))
    windows = jnp.concatenate([above, edge, below], axis=1).astype(bf16)
    product = jnp.dot(windows, weight, preferred_element_type=f32)
    return product.reshape(length, ROWS, 3 * C)


def edge_sum(valid_ref, product_ref, frame):
    return (
        product_ref[frame, :, 0:C]
        + valid_ref[0, frame] * product_ref[frame - 1, :, C : 2 * C]
        + valid_ref[1, frame] * product_ref[frame - 2, :, 2 * C :]
    )


def group_total(entries):
    lane = lax.broadcasted_iota(jnp.int32, entries.shape, 1)
    for bit in (1, 2):
        up = pltpu.roll(entries, C - bit, 1)
        down = pltpu.roll(entries, bit, 1)
        entries = entries + jnp.where((lane & bit) == 0, up, down)
    return entries


HALF = 24


def precise_dot(a, b):
    return jnp.dot(a, b, precision=lax.Precision.HIGHEST, preferred_element_type=f32)


def stats_kernel(
    valid_ref, partial_ref, left_ref, right_ref, wl_ref, wr_ref, out_ref, stats_ref,
    product_l, product_r, means, spreads,
):
    length = partial_ref.shape[0]
    product_l[...] = edge_product(left_ref, wl_ref[...])
    product_r[...] = edge_product(right_ref, wr_ref[...])
    out_ref[0:2] = jnp.zeros((2, POS, C), f32)
    means[...] = jnp.zeros_like(means)
    spreads[...] = jnp.zeros_like(spreads)

    def step(pair, carry):
        for q in range(2):
            frame = 2 + pair * 2 + q
            out_ref[frame] = partial_ref[frame]
            at_left = pl.ds(0, ROWS, stride=COLS)
            at_right = pl.ds(COLS - 1, ROWS, stride=COLS)
            out_ref[frame, at_left, :] += edge_sum(valid_ref, product_l, frame)
            out_ref[frame, at_right, :] += edge_sum(valid_ref, product_r, frame)
            hidden = out_ref[frame]
            mean = jnp.sum(hidden, axis=0, keepdims=True) / POS
            centred = hidden - mean
            means[pl.ds(frame, 1), :] = mean
            spreads[pl.ds(frame, 1), :] = jnp.sum(centred * centred, axis=0, keepdims=True)
        return carry

    lax.fori_loop(0, (length - 2) // 2, step, 0)
    mean = group_total(means[...]) / 4
    off = means[...] - mean
    spread = group_total(spreads[...] + POS * off * off)
    channel = lax.broadcasted_iota(jnp.int32, (C, C), 0)
    lane = lax.broadcasted_iota(jnp.int32, (C, C), 1)
    packed = jnp.zeros((HALF, C), f32)
    for q, part in enumerate((mean[:HALF], spread[:HALF], mean[HALF:], spread[HALF:])):
        picks = (channel == 4 * (lane - GROUPS * q)) & (lane // GROUPS == q)
        packed = packed + precise_dot(part, picks.astype(f32))
    for peer in range(stats_ref.shape[0]):
        stats_ref[peer] = packed


def finish_hidden(valid, partial, left, right, wl, wr, tiles):
    length = partial.shape[0]
    return pl.pallas_call(
        stats_kernel,
        out_shape=(
            jax.ShapeDtypeStruct(partial.shape, f32),
            jax.ShapeDtypeStruct((tiles, HALF, C), f32),
        ),
        in_specs=[smem()] + [vmem()] * 5,
        out_specs=(vmem(), vmem()),
        scratch_shapes=[
            pltpu.VMEM((length, ROWS, 3 * C), f32),
            pltpu.VMEM((length, ROWS, 3 * C), f32),
            pltpu.VMEM((2 * HALF, C), f32),
            pltpu.VMEM((2 * HALF, C), f32),
        ],
        compiler_params=params(),
        name="finish_hidden",
    )(valid, partial, left, right, wl, wr)


def norm_kernel(
    hidden_ref, stats_ref, gain_ref, bias_ref, active_ref, left_ref, right_ref,
    means, scales, wide,
):
    length = hidden_ref.shape[0]
    tiles = stats_ref.shape[0]
    here = POS * (C // GROUPS)
    lane = lax.broadcasted_iota(jnp.int32, (HALF, C), 1)
    is_mean = (lane // GROUPS) % 2 == 0
    total = stats_ref[0]
    for peer in range(1, tiles):
        total = total + stats_ref[peer]
    mean = total / tiles
    apart = jnp.zeros((HALF, C), f32)
    for peer in range(tiles):
        off = stats_ref[peer] - mean
        apart = apart + off * off
    apart = jnp.where(is_mean, apart, 0.0)
    variance = (total + here * pltpu.roll(apart, GROUPS, 1)) / (here * tiles)
    packed = jnp.where(is_mean, mean, lax.rsqrt(jnp.where(is_mean, 1.0, variance) + EPSILON))
    channel = lax.broadcasted_iota(jnp.int32, (C, C), 1)
    source = lax.broadcasted_iota(jnp.int32, (C, C), 0)
    spread_out = []
    for q in range(4):
        picks = (source == channel // (C // GROUPS) + GROUPS * q).astype(f32)
        spread_out.append(precise_dot(packed, picks))
    means[0:HALF] = spread_out[0]
    means[HALF:] = spread_out[2]
    scales[0:HALF] = spread_out[1]
    scales[HALF:] = spread_out[3]
    scales[...] = scales[...] * gain_ref[...]
    active_ref[0:2] = jnp.zeros((2, ROWS, COLS, C), bf16)
    left_ref[0:2] = jnp.zeros((2, ROWS, C), bf16)
    right_ref[0:2] = jnp.zeros((2, ROWS, C), bf16)

    def step(pair, carry):
        for q in range(2):
            frame = 2 + pair * 2 + q
            centred = hidden_ref[frame] - means[pl.ds(frame, 1), :]
            normed = centred * scales[pl.ds(frame, 1), :] + bias_ref[...]
            active = normed * (1.0 / (1.0 + jnp.exp(-normed)))
            wide[q] = active
            active_ref[frame] = active.astype(bf16).reshape(ROWS, COLS, C)
            left_ref[frame] = wide[q, pl.ds(0, ROWS, stride=COLS), :].astype(bf16)
            right_ref[frame] = wide[q, pl.ds(COLS - 1, ROWS, stride=COLS), :].astype(bf16)
        return carry

    lax.fori_loop(0, (length - 2) // 2, step, 0)


def norm_silu(hidden, stats, gain, bias):
    length = hidden.shape[0]
    edge = jax.ShapeDtypeStruct((length, ROWS, C), bf16)
    return pl.pallas_call(
        norm_kernel,
        out_shape=(jax.ShapeDtypeStruct((length, ROWS, COLS, C), bf16), edge, edge),
        in_specs=[vmem()] * 4,
        out_specs=(vmem(),) * 3,
        scratch_shapes=[
            pltpu.VMEM((2 * HALF, C), f32),
            pltpu.VMEM((2 * HALF, C), f32),
            pltpu.VMEM((2, POS, C), f32),
        ],
        compiler_params=params(),
        name="norm_silu",
    )(hidden, stats, gain, bias)


def output_kernel(
    valid_ref, partial_ref, left_ref, right_ref, wl_ref, wr_ref, frames_ref, bias_ref, out_ref,
    product_l, product_r, wide,
):
    product_l[...] = edge_product(left_ref, wl_ref[...])
    product_r[...] = edge_product(right_ref, wr_ref[...])

    def step(pair, carry):
        for q in range(2):
            frame = LEAD + pair * 2 + q
            wide[q] = partial_ref[frame] + bias_ref[...]
            at_left = pl.ds(0, ROWS, stride=COLS)
            at_right = pl.ds(COLS - 1, ROWS, stride=COLS)
            wide[q, at_left, :] += edge_sum(valid_ref, product_l, frame)
            wide[q, at_right, :] += edge_sum(valid_ref, product_r, frame)
            total = frames_ref[frame].reshape(POS, C).astype(f32) + wide[q]
            out_ref[frame - LEAD] = total.astype(bf16).reshape(ROWS, COLS, C)
        return carry

    lax.fori_loop(0, out_ref.shape[0] // 2, step, 0)


def finish_output(valid, partial, left, right, wl, wr, frames, bias):
    length = partial.shape[0]
    return pl.pallas_call(
        output_kernel,
        out_shape=jax.ShapeDtypeStruct((length - LEAD, ROWS, COLS, C), bf16),
        in_specs=[smem()] + [vmem()] * 7,
        out_specs=vmem(),
        scratch_shapes=[
            pltpu.VMEM((length, ROWS, 3 * C), f32),
            pltpu.VMEM((length, ROWS, 3 * C), f32),
            pltpu.VMEM((2, POS, C), f32),
        ],
        compiler_params=params(),
        name="finish_output",
    )(valid, partial, left, right, wl, wr, frames, bias)


def block_order(all_slots, position):
    owner_of = jnp.where(all_slots >= 0, all_slots >> 4, -1)
    slot_ids = jnp.arange(all_slots.shape[1], dtype=jnp.int32)
    precedes = (owner_of[:, None, :] == owner_of[:, :, None]) & (
        slot_ids[None, None, :] < slot_ids[None, :, None]
    )
    rank = jnp.sum(precedes.astype(jnp.int32), axis=2)
    sources = jnp.arange(all_slots.shape[0], dtype=jnp.int32)
    arrival = sources[:, None] * CAP + rank
    wanted = position * OWN + jnp.arange(OWN, dtype=jnp.int32)
    matches = all_slots[None] == wanted[:, None, None]
    return jnp.sum(jnp.where(matches, arrival[None], 0), axis=(1, 2))


def lag_masks(clip_frames, first_frame, length):
    clip_ends = jnp.cumsum(clip_frames)

    def clip_of(frames):
        ids = jnp.sum((frames[:, None] >= clip_ends[None, :]).astype(jnp.int32), axis=1)
        return jnp.where(frames < 0, -1, ids)

    frames = first_frame + jnp.arange(length, dtype=jnp.int32)
    here = clip_of(frames)
    return jnp.stack([clip_of(frames - lag) == here for lag in (1, 2)]).astype(f32)


def lag_weight(weight):
    lags = weight[::-1].transpose(2, 1, 3, 0, 4)
    return lags.reshape(9 * C, 3 * C)


def swap_edges(left, right):
    count = lax.axis_size("tile")
    from_left = lax.ppermute(right, "tile", [(i, i + 1) for i in range(count - 1)])
    from_right = lax.ppermute(left, "tile", [(i + 1, i) for i in range(count - 1)])
    return from_left, from_right


def shards(
    video, slot_block, clip_frames, conv1_weight, norm_gain, norm_bias, conv2_weight, conv2_bias
):
    owners = lax.axis_size("tm")
    tiles = lax.axis_size("tile")
    position = lax.axis_index("tm")
    length = OWN * video.shape[1]

    all_slots = lax.all_gather(slot_block, "tm")
    outgoing = send_blocks(slot_block, video, owners)
    outgoing = outgoing.reshape((owners, CAP) + video.shape[1:])
    arrived = lax.all_to_all(outgoing, "tm", split_axis=0, concat_axis=0, tiled=True)
    arrived = arrived.reshape((owners * CAP,) + video.shape[1:])

    valid = lag_masks(clip_frames, position * length - LEAD, length + LEAD)
    weight1 = lag_weight(conv1_weight)
    weight2 = lag_weight(conv2_weight)
    order = block_order(all_slots, position)

    tail = jnp.take(arrived, order[OWN - LEAD // 2 :], axis=0).reshape((LEAD,) + video.shape[2:])
    lead = lax.ppermute(tail, "tm", [(i, i + 1) for i in range(owners - 1)])
    frames, left, right = place_blocks(order, arrived, lead)
    from_left, from_right = swap_edges(left, right)
    partial = conv(valid, frames, weight1)
    hidden, stats = finish_hidden(
        valid, partial, from_left, from_right, weight1[: 3 * C], weight1[6 * C :], tiles
    )
    stats = lax.all_to_all(stats, "tile", split_axis=0, concat_axis=0, tiled=True)
    active, left, right = norm_silu(hidden, stats, norm_gain[None], norm_bias[None])
    from_left, from_right = swap_edges(left, right)
    partial = conv(valid, active, weight2)
    return finish_output(
        valid, partial, from_left, from_right, weight2[: 3 * C], weight2[6 * C :], frames,
        conv2_bias[None],
    )


def solution(mesh):
    placed = (P("tm", None, None, "tile", None), P("tm"), P(), P(), P(), P(), P(), P())
    return jax.shard_map(
        shards, mesh=mesh, in_specs=placed, out_specs=P("tm", None, "tile", None), check_vma=False
    )
```

```python
import functools

import jax
import jax.numpy as jnp
from jax import lax
from jax.experimental import pallas as pl
from jax.experimental.pallas import tpu as pltpu
from jax.sharding import PartitionSpec as P

GROUPS = 32
OWN = 16
CAP = 2
C = 128
ROWS = 8
COLS = 16
POS = ROWS * COLS
LEAD = 4
CHUNK = 4
EPSILON = 1e-06
HALF = 24
PITCH = 24
UNROLL = 8
PAIR_ROWS = CAP * 2 * POS
INFO_ROWS = 16
MIB = 1024 * 1024

f32 = jnp.float32
bf16 = jnp.bfloat16


def vmem():
    return pl.BlockSpec(memory_space=pltpu.VMEM)


def smem():
    return pl.BlockSpec(memory_space=pltpu.SMEM)


def hbm():
    return pl.BlockSpec(memory_space=pl.ANY)


def params(mib=16):
    return pltpu.CompilerParams(vmem_limit_bytes=mib * MIB)


def hbm_only():
    return pl.BlockSpec(memory_space=pltpu.HBM)


def send_kernel(slot_ref, video_ref, out_ref, count, info, info_out, sems):
    slots = slot_ref.shape[0]
    owners = count.shape[0]
    for owner in range(owners):
        count[owner] = 0
    info[...] = jnp.zeros_like(info)
    lane = lax.broadcasted_iota(jnp.int32, info.shape[1:], 1)

    def copy(slot, owner, rank):
        block_rows = PAIR_ROWS // CAP
        rows = pl.ds(pl.multiple_of(rank * block_rows, block_rows), block_rows)
        return pltpu.make_async_copy(
            video_ref.at[slot], out_ref.at[owner, rows], sems.at[slot]
        )

    for slot in range(slots):
        block = slot_ref[slot]

        @pl.when(block >= 0)
        def _():
            owner = block >> 4
            rank = count[owner]
            count[owner] = rank + 1
            copy(slot, owner, rank).start()
            mark = jnp.where(lane == (block & (OWN - 1)), (rank + 1).astype(f32), 0.0)
            info[owner] = info[owner] + mark

    for owner in range(owners):
        info_out[owner] = jnp.concatenate([info[owner]] * 2, axis=0).astype(bf16)
    notes = pltpu.make_async_copy(
        info_out, out_ref.at[:, pl.ds(PAIR_ROWS, INFO_ROWS)], sems.at[slots]
    )
    notes.start()
    for slot in range(slots):

        @pl.when(slot_ref[slot] >= 0)
        def _():
            copy(slot, 0, 0).wait()

    notes.wait()


def send_blocks(slot_block, video, owners):
    slots = video.shape[0]
    return pl.pallas_call(
        send_kernel,
        out_shape=jax.ShapeDtypeStruct((owners, PAIR_ROWS + INFO_ROWS, C), video.dtype),
        in_specs=[smem(), hbm_only()],
        out_specs=hbm_only(),
        scratch_shapes=[
            pltpu.SMEM((owners,), jnp.int32),
            pltpu.VMEM((owners, 8, C), f32),
            pltpu.VMEM((owners, INFO_ROWS, C), bf16),
            pltpu.SemaphoreType.DMA((slots + 1,)),
        ],
        compiler_params=params(62),
        name="send_blocks",
    )(slot_block, video.reshape(slots, PAIR_ROWS // CAP, C))


def order_kernel(arrived_ref, order_ref, tail_ref, notes, picks, sems):
    owners = arrived_ref.shape[0]
    note = pltpu.make_async_copy(
        arrived_ref.at[:, pl.ds(PAIR_ROWS, INFO_ROWS)], notes, sems.at[0]
    )
    note.start()
    note.wait()
    total = jnp.zeros((8, C), f32)
    for source in range(owners):
        rank = notes[source].astype(f32)[0:8]
        total = total + jnp.where(rank > 0.0, rank + (CAP * source - 1.0), 0.0)
    picks[...] = total.astype(jnp.int32)
    to_scalars = pltpu.make_async_copy(picks.at[pl.ds(0, 1)], order_ref, sems.at[0])
    to_scalars.start()
    to_scalars.wait()
    copies = []
    for k in range(LEAD // 2):
        copies.append(
            pltpu.make_async_copy(
                block_at(arrived_ref, order_ref[0, OWN - LEAD // 2 + k]),
                tail_ref.at[pl.ds(k * 2 * POS, 2 * POS)],
                sems.at[k],
            )
        )
        copies[-1].start()
    for copy in copies:
        copy.wait()


def block_at(arrived_ref, arrival):
    block_rows = PAIR_ROWS // CAP
    rows = pl.ds(pl.multiple_of((arrival & 1) * block_rows, block_rows), block_rows)
    return arrived_ref.at[arrival >> 1, rows]


def block_order(arrived):
    return pl.pallas_call(
        order_kernel,
        out_shape=(
            jax.ShapeDtypeStruct((1, C), jnp.int32),
            jax.ShapeDtypeStruct((LEAD * POS, C), bf16),
        ),
        in_specs=[hbm_only()],
        out_specs=(smem(), vmem()),
        scratch_shapes=[
            pltpu.VMEM((arrived.shape[0], INFO_ROWS, C), bf16),
            pltpu.VMEM((8, C), jnp.int32),
            pltpu.SemaphoreType.DMA((LEAD // 2,)),
        ],
        compiler_params=params(),
        name="block_order",
    )(arrived)


def edge_rows(wide, column):
    return wide[pl.ds(column, wide.shape[0] // COLS, stride=COLS), :]


EDGE_ROWS = (LEAD + 2 * OWN) * ROWS


def put_edges(wide, start, left_ref, right_ref):
    count = wide.shape[0] // COLS
    for c in range(2):
        at = pl.ds(c * EDGE_ROWS + start, count)
        left_ref[at] = edge_rows(wide, c).astype(bf16)
        right_ref[at] = edge_rows(wide, COLS - 2 + c).astype(bf16)


def place_kernel(order_ref, arrived_ref, frames_ref, left_ref, right_ref, wide, sems):
    copies = [
        pltpu.make_async_copy(
            block_at(arrived_ref, order_ref[0, k]),
            frames_ref.at[pl.ds(k * 2 * POS, 2 * POS)],
            sems.at[k],
        )
        for k in range(OWN)
    ]
    for copy in copies:
        copy.start()
    for k in range(OWN):
        copies[k].wait()
        wide[k % 2] = frames_ref[k * 2 * POS : (k + 1) * 2 * POS].astype(f32)
        put_edges(wide.at[k % 2], (LEAD + 2 * k) * ROWS, left_ref, right_ref)


def edge_shape(dtype):
    return jax.ShapeDtypeStruct((2 * EDGE_ROWS, C), dtype)


def place_blocks(order, arrived):
    edge = edge_shape(bf16)
    return pl.pallas_call(
        place_kernel,
        out_shape=(jax.ShapeDtypeStruct((2 * OWN * POS, C), bf16), edge, edge),
        in_specs=[smem(), hbm_only()],
        out_specs=(vmem(), vmem(), vmem()),
        scratch_shapes=[
            pltpu.VMEM((2, 2 * POS, C), f32),
            pltpu.SemaphoreType.DMA((OWN,)),
        ],
        compiler_params=params(),
        name="place_blocks",
    )(order, arrived)


def lead_kernel(lead_ref, left_in, right_in, left_ref, right_ref, wide):
    wide[...] = lead_ref[...].astype(f32)
    left_ref[...] = left_in[...]
    right_ref[...] = right_in[...]
    put_edges(wide, 0, left_ref, right_ref)


def lead_edges(lead, left, right):
    edge = edge_shape(bf16)
    return pl.pallas_call(
        lead_kernel,
        out_shape=(edge, edge),
        in_specs=[vmem()] * 3,
        out_specs=(vmem(), vmem()),
        scratch_shapes=[pltpu.VMEM((LEAD * POS, C), f32)],
        compiler_params=params(),
        name="lead_edges",
    )(lead, left, right)


def join_weight(weight_ref, joined):
    for j in range(3):
        for i in range(3):
            for lag in range(3):
                at = (3 * j + i) * C
                joined[at : at + C, lag * C : (lag + 1) * C] = weight_ref[2 - lag, i, j]


def conv_chunk(valid_ref, start, count, wide, taps, joined, carry, sides):
    rows = count * ROWS
    for at in range(rows):
        q, r = at // ROWS, at % ROWS + 1
        base = at * PITCH + 8
        for j in range(3):
            taps[j, q, r] = wide[base + j - 1 : base + j - 1 + COLS].astype(bf16)
    pieces = [
        taps[j, 0:count, i : i + ROWS].reshape(count * POS, C) for j in range(3) for i in range(3)
    ]
    if sides:
        row = lax.broadcasted_iota(jnp.int32, (2 * rows, C), 0) % ROWS
        for j in range(3):
            column = jnp.concatenate(
                [wide[pl.ds(at + j, rows, stride=PITCH), :] for at in (6, 7 + COLS)], axis=0
            )
            above = jnp.where(row == 0, 0.0, pltpu.roll(column, 1, 0))
            below = jnp.where(row == ROWS - 1, 0.0, pltpu.roll(column, 2 * rows - 1, 0))
            for i, piece in enumerate((above, column, below)):
                at = 3 * j + i
                pieces[at] = jnp.concatenate([pieces[at], piece.astype(bf16)], axis=0)
    product = jnp.dot(
        jnp.concatenate(pieces, axis=1), joined[...], preferred_element_type=f32
    )

    def part(q, lag):
        lanes = slice(lag * C, (lag + 1) * C)
        own = product[q * POS : (q + 1) * POS, lanes]
        if not sides:
            return own
        left = count * POS + q * ROWS
        right = left + rows
        edges = [product[at : at + ROWS, lanes] for at in (left, right)]
        return jnp.concatenate([own] + edges, axis=0)

    totals = []
    for q in range(count):
        one = part(q - 1, 1) if q >= 1 else carry[0]
        two = part(q - 2, 2) if q >= 2 else carry[1 + q]
        totals.append(
            part(q, 0) + valid_ref[0, start + q] * one + valid_ref[1, start + q] * two
        )
    carry[0] = part(count - 1, 1)
    carry[1] = part(count - 2, 2)
    carry[2] = part(count - 1, 2)
    return totals


def conv_scratch(sides):
    return [
        pltpu.VMEM((UNROLL, CHUNK * ROWS * PITCH + 8, C), f32),
        pltpu.VMEM((UNROLL, 3, CHUNK, ROWS + 2, COLS, C), bf16),
        pltpu.VMEM((9 * C, 3 * C), bf16),
        pltpu.VMEM((3, POS + (2 * ROWS if sides else 0), C), f32),
    ]


def conv_setup(weight_ref, taps, joined, carry):
    join_weight(weight_ref, joined)
    carry[...] = jnp.zeros_like(carry)
    for u in range(UNROLL):
        for j in range(3):
            for edge in (0, ROWS + 1):
                taps[u, j, :, edge] = jnp.zeros((CHUNK, COLS, C), bf16)


def put_column(wide, at, column):
    wide[pl.ds(at, column.shape[0], stride=PITCH), :] = column


def over_chunks(chunk_step):
    def step(trip, done):
        for u in range(UNROLL):
            chunk_step(u, (trip * UNROLL + u) * CHUNK)
        return done

    lax.fori_loop(0, 2 * OWN // CHUNK // UNROLL, step, 0)


def group_total(entries):
    lane = lax.broadcasted_iota(jnp.int32, entries.shape, 1)
    for bit in (1, 2):
        up = pltpu.roll(entries, C - bit, 1)
        down = pltpu.roll(entries, bit, 1)
        entries = entries + jnp.where((lane & bit) == 0, up, down)
    return entries


def precise_dot(a, b):
    return jnp.dot(a, b, precision=lax.Precision.HIGHEST, preferred_element_type=f32)


def hidden_kernel(
    valid_ref, lead_ref, frames_ref, left_ref, right_ref, weight_ref,
    hidden_ref, edge_l_ref, edge_r_ref, stats_ref,
    wide, taps, joined, carry, means, spreads,
):
    conv_setup(weight_ref, taps, joined, carry)
    means[...] = jnp.zeros_like(means)
    spreads[...] = jnp.zeros_like(spreads)

    def chunk_step(u, start, count, source, at):
        for row in range(count * ROWS):
            here = source[pl.ds(pl.multiple_of(at + row * COLS, COLS), COLS)]
            wide[u, row * PITCH + 8 : row * PITCH + 8 + COLS] = here.astype(f32)
        for c in range(2):
            edge_at = pl.multiple_of(c * EDGE_ROWS + start * ROWS, 2 * ROWS)
            edge_at = pl.ds(edge_at, count * ROWS)
            put_column(wide.at[u], 6 + c, left_ref[edge_at].astype(f32))
            put_column(wide.at[u], 8 + COLS + c, right_ref[edge_at].astype(f32))
        totals = conv_chunk(
            valid_ref, start, count, wide.at[u], taps.at[u], joined, carry, True
        )
        for q in range(count):
            frame = start + q
            own = totals[q][:POS]
            hidden_ref[frame] = own
            edge_l_ref[frame] = totals[q][POS : POS + ROWS]
            edge_r_ref[frame] = totals[q][POS + ROWS :]
            mean = jnp.sum(own, axis=0, keepdims=True) / POS
            centred = own - mean
            means[pl.ds(frame, 1), :] = mean
            spreads[pl.ds(frame, 1), :] = jnp.sum(centred * centred, axis=0, keepdims=True)

    for start in range(0, LEAD, CHUNK):
        chunk_step(0, start, min(CHUNK, LEAD), lead_ref, start * POS)
    over_chunks(lambda u, at: chunk_step(u, LEAD + at, CHUNK, frames_ref, at * POS))

    mean = group_total(means[...]) / 4
    off = means[...] - mean
    spread = group_total(spreads[...] + POS * off * off)
    channel = lax.broadcasted_iota(jnp.int32, (C, C), 0)
    lane = lax.broadcasted_iota(jnp.int32, (C, C), 1)
    packed = jnp.zeros((HALF, C), f32)
    for q, part in enumerate((mean[:HALF], spread[:HALF], mean[HALF:], spread[HALF:])):
        picks = (channel == 4 * (lane - GROUPS * q)) & (lane // GROUPS == q)
        packed = packed + precise_dot(part, picks.astype(f32))
    for peer in range(stats_ref.shape[0]):
        stats_ref[peer] = packed


def first_layer(valid, lead, frames, left, right, weight, tiles):
    length = LEAD + 2 * OWN
    edge = jax.ShapeDtypeStruct((length, ROWS, C), f32)
    return pl.pallas_call(
        hidden_kernel,
        out_shape=(
            jax.ShapeDtypeStruct((length, POS, C), f32),
            edge,
            edge,
            jax.ShapeDtypeStruct((tiles, HALF, C), f32),
        ),
        in_specs=[smem()] + [vmem()] * 5,
        out_specs=(vmem(),) * 4,
        scratch_shapes=conv_scratch(True)
        + [pltpu.VMEM((2 * HALF, C), f32), pltpu.VMEM((2 * HALF, C), f32)],
        compiler_params=params(),
        name="first_layer",
    )(valid, lead, frames, left, right, weight)


def combine_stats(stats_ref, gain_ref, means, scales):
    tiles = stats_ref.shape[0]
    here = POS * (C // GROUPS)
    lane = lax.broadcasted_iota(jnp.int32, (HALF, C), 1)
    is_mean = (lane // GROUPS) % 2 == 0
    total = stats_ref[0]
    for peer in range(1, tiles):
        total = total + stats_ref[peer]
    mean = total / tiles
    apart = jnp.zeros((HALF, C), f32)
    for peer in range(tiles):
        off = stats_ref[peer] - mean
        apart = apart + off * off
    apart = jnp.where(is_mean, apart, 0.0)
    variance = (total + here * pltpu.roll(apart, GROUPS, 1)) / (here * tiles)
    packed = jnp.where(is_mean, mean, lax.rsqrt(jnp.where(is_mean, 1.0, variance) + EPSILON))
    channel = lax.broadcasted_iota(jnp.int32, (C, C), 1)
    source = lax.broadcasted_iota(jnp.int32, (C, C), 0)
    for q in range(4):
        picks = (source == channel // (C // GROUPS) + GROUPS * q).astype(f32)
        target = scales if q % 2 else means
        half = pl.ds((q // 2) * HALF, HALF)
        target[half, :] = precise_dot(packed, picks)
    scales[...] = scales[...] * gain_ref[...]


def silu(v):
    return v * (1.0 / (1.0 + jnp.exp(-v)))


def output_kernel(
    valid_ref, hidden_ref, edge_l_ref, edge_r_ref, stats_ref, frames_ref,
    gain_ref, norm_bias_ref, weight_ref, bias_ref, out_ref,
    wide, taps, joined, carry, means, scales, halo,
):
    conv_setup(weight_ref, taps, joined, carry)
    combine_stats(stats_ref, gain_ref, means, scales)
    has_left = valid_ref[2, 0]
    has_right = valid_ref[2, 1]

    def norm(hidden, frame):
        centred = hidden - means[pl.ds(frame, 1), :]
        return silu(centred * scales[pl.ds(frame, 1), :] + norm_bias_ref[...])

    def chunk_step(u, start, count):
        for q in range(count):
            frame = start + q
            active = norm(hidden_ref[frame], frame)
            for r in range(ROWS):
                at = (q * ROWS + r) * PITCH + 8
                wide[u, at : at + COLS] = active[r * COLS : (r + 1) * COLS]
            halo[u, 0, q * ROWS : (q + 1) * ROWS] = norm(edge_l_ref[frame], frame) * has_left
            halo[u, 1, q * ROWS : (q + 1) * ROWS] = norm(edge_r_ref[frame], frame) * has_right
        put_column(wide.at[u], 7, halo[u, 0, 0 : count * ROWS])
        put_column(wide.at[u], 8 + COLS, halo[u, 1, 0 : count * ROWS])
        return conv_chunk(
            valid_ref, start, count, wide.at[u], taps.at[u], joined, carry, False
        )

    def own_chunk(u, start):
        totals = chunk_step(u, LEAD + start, CHUNK)
        for q in range(CHUNK):
            rows = pl.ds(pl.multiple_of((start + q) * POS, POS), POS)
            total = frames_ref[rows].astype(f32) + (totals[q] + bias_ref[...])
            out_ref[rows] = total.astype(bf16)

    chunk_step(0, LEAD - 2, 2)
    over_chunks(own_chunk)


def second_layer(valid, hidden, edge_l, edge_r, stats, frames, gain, norm_bias, weight, bias):
    return pl.pallas_call(
        output_kernel,
        out_shape=jax.ShapeDtypeStruct(frames.shape, bf16),
        in_specs=[smem()] + [vmem()] * 9,
        out_specs=vmem(),
        scratch_shapes=conv_scratch(False)
        + [
            pltpu.VMEM((2 * HALF, C), f32),
            pltpu.VMEM((2 * HALF, C), f32),
            pltpu.VMEM((UNROLL, 2, CHUNK * ROWS, C), f32),
        ],
        compiler_params=params(),
        name="second_layer",
    )(valid, hidden, edge_l, edge_r, stats, frames, gain, norm_bias, weight, bias)


def lag_masks(clip_frames, first_frame, length):
    clip_ends = jnp.cumsum(clip_frames)

    def clip_of(frames):
        ids = jnp.sum((frames[:, None] >= clip_ends[None, :]).astype(jnp.int32), axis=1)
        return jnp.where(frames < 0, -1, ids)

    frames = first_frame + jnp.arange(length, dtype=jnp.int32)
    here = clip_of(frames)
    return jnp.stack([clip_of(frames - lag) == here for lag in (1, 2)])


def swap_edges(left, right):
    count = lax.axis_size("tile")
    from_left = lax.ppermute(right, "tile", [(i, i + 1) for i in range(count - 1)])
    from_right = lax.ppermute(left, "tile", [(i + 1, i) for i in range(count - 1)])
    return from_left, from_right


def shards(
    video, slot_block, clip_frames, conv1_weight, norm_gain, norm_bias, conv2_weight, conv2_bias
):
    owners = lax.axis_size("tm")
    tiles = lax.axis_size("tile")
    position = lax.axis_index("tm")
    tile = lax.axis_index("tile")
    length = 2 * OWN

    outgoing = send_blocks(slot_block, video, owners)
    arrived = lax.all_to_all(outgoing, "tm", split_axis=0, concat_axis=0, tiled=True)

    inside = jnp.stack([tile > 0, tile < tiles - 1] + [tile < 0] * (length + LEAD - 2))
    valid = jnp.concatenate(
        [lag_masks(clip_frames, position * length - LEAD, length + LEAD), inside[None]]
    ).astype(f32)

    order, tail = block_order(arrived)
    lead = lax.ppermute(tail, "tm", [(i, i + 1) for i in range(owners - 1)])
    frames, left, right = place_blocks(order, arrived)
    left, right = lead_edges(lead, left, right)
    from_left, from_right = swap_edges(left, right)
    hidden, edge_l, edge_r, stats = first_layer(
        valid, lead, frames, from_left, from_right, conv1_weight, tiles
    )
    stats = lax.all_to_all(stats, "tile", split_axis=0, concat_axis=0, tiled=True)
    encoded = second_layer(
        valid, hidden, edge_l, edge_r, stats, frames, norm_gain[None], norm_bias[None],
        conv2_weight, conv2_bias[None],
    )
    return encoded.reshape((length,) + video.shape[2:])


def solution(mesh):
    placed = (P("tm", None, None, "tile", None), P("tm"), P(), P(), P(), P(), P(), P())
    return jax.shard_map(
        shards, mesh=mesh, in_specs=placed, out_specs=P("tm", None, "tile", None), check_vma=False
    )
```

```python
import functools

import jax
import jax.numpy as jnp
from jax import lax
from jax.experimental import pallas as pl
from jax.experimental.pallas import tpu as pltpu
from jax.sharding import PartitionSpec as P

GROUPS = 32
OWN = 16
CAP = 2
C = 128
ROWS = 8
COLS = 16
POS = ROWS * COLS
LEAD = 4
CHUNK = 4
EPSILON = 1e-06
HALF = 24
PITCH = 24
UNROLL = 8
PAIR_ROWS = CAP * 2 * POS
INFO_ROWS = 16
MIB = 1024 * 1024

f32 = jnp.float32
bf16 = jnp.bfloat16


def vmem():
    return pl.BlockSpec(memory_space=pltpu.VMEM)


def smem():
    return pl.BlockSpec(memory_space=pltpu.SMEM)


def hbm():
    return pl.BlockSpec(memory_space=pl.ANY)


def params(mib=16):
    return pltpu.CompilerParams(vmem_limit_bytes=mib * MIB)


def hbm_only():
    return pl.BlockSpec(memory_space=pltpu.HBM)


def send_kernel(slot_ref, video_ref, out_ref, count, held, info, info_out, sems_in, sems_out):
    slots = slot_ref.shape[0]
    owners = count.shape[0]
    block_rows = PAIR_ROWS // CAP

    def load(slot):
        return pltpu.make_async_copy(video_ref.at[slot], held.at[slot], sems_in.at[slot])

    def store(slot, owner, rank):
        rows = pl.ds(pl.multiple_of(rank * block_rows, block_rows), block_rows)
        return pltpu.make_async_copy(
            held.at[slot], out_ref.at[owner, rows], sems_out.at[slot]
        )

    for slot in range(slots):

        @pl.when(slot_ref[slot] >= 0)
        def _():
            load(slot).start()

    for owner in range(owners):
        count[owner] = 0
    info[...] = jnp.zeros_like(info)
    lane = lax.broadcasted_iota(jnp.int32, info.shape[1:], 1)
    for slot in range(slots):
        block = slot_ref[slot]

        @pl.when(block >= 0)
        def _():
            owner = block >> 4
            rank = count[owner]
            count[owner] = rank + 1
            mark = jnp.where(lane == (block & (OWN - 1)), (rank + 1).astype(f32), 0.0)
            info[owner] = info[owner] + mark
            load(slot).wait()
            store(slot, owner, rank).start()

    for owner in range(owners):
        info_out[owner] = jnp.concatenate([info[owner]] * 2, axis=0).astype(bf16)
    notes = pltpu.make_async_copy(
        info_out, out_ref.at[:, pl.ds(PAIR_ROWS, INFO_ROWS)], sems_out.at[slots]
    )
    notes.start()
    for slot in range(slots):

        @pl.when(slot_ref[slot] >= 0)
        def _():
            store(slot, 0, 0).wait()

    notes.wait()


def send_blocks(slot_block, video, owners):
    slots = video.shape[0]
    return pl.pallas_call(
        send_kernel,
        out_shape=jax.ShapeDtypeStruct((owners, PAIR_ROWS + INFO_ROWS, C), video.dtype),
        in_specs=[smem(), hbm_only()],
        out_specs=hbm_only(),
        scratch_shapes=[
            pltpu.SMEM((owners,), jnp.int32),
            pltpu.VMEM((slots, PAIR_ROWS // CAP, C), bf16),
            pltpu.VMEM((owners, 8, C), f32),
            pltpu.VMEM((owners, INFO_ROWS, C), bf16),
            pltpu.SemaphoreType.DMA((slots,)),
            pltpu.SemaphoreType.DMA((slots + 1,)),
        ],
        compiler_params=params(62),
        name="send_blocks",
    )(slot_block, video.reshape(slots, PAIR_ROWS // CAP, C))


def order_kernel(arrived_ref, *refs):
    order_ref, tail_ref, notes, picks, sems = refs[-5:]
    owners = arrived_ref.shape[0]
    note = pltpu.make_async_copy(
        arrived_ref.at[:, pl.ds(PAIR_ROWS, INFO_ROWS)], notes, sems.at[0]
    )
    note.start()
    note.wait()
    total = jnp.zeros((8, C), f32)
    for source in range(owners):
        rank = notes[source].astype(f32)[0:8]
        total = total + jnp.where(rank > 0.0, rank + (CAP * source - 1.0), 0.0)
    picks[...] = total.astype(jnp.int32)
    to_scalars = pltpu.make_async_copy(picks.at[pl.ds(0, 1)], order_ref, sems.at[0])
    to_scalars.start()
    to_scalars.wait()
    copies = []
    for k in range(LEAD // 2):
        copies.append(
            pltpu.make_async_copy(
                block_at(arrived_ref, order_ref[0, OWN - LEAD // 2 + k]),
                tail_ref.at[pl.ds(k * 2 * POS, 2 * POS)],
                sems.at[k],
            )
        )
        copies[-1].start()
    for copy in copies:
        copy.wait()


def block_at(arrived_ref, arrival):
    block_rows = PAIR_ROWS // CAP
    rows = pl.ds(pl.multiple_of((arrival & 1) * block_rows, block_rows), block_rows)
    return arrived_ref.at[arrival >> 1, rows]


def block_order(arrived, ready):
    return pl.pallas_call(
        order_kernel,
        out_shape=(
            jax.ShapeDtypeStruct((1, C), jnp.int32),
            jax.ShapeDtypeStruct((LEAD * POS, C), bf16),
        ),
        in_specs=[hbm_only()] + [hbm()] * len(ready),
        out_specs=(smem(), vmem()),
        scratch_shapes=[
            pltpu.VMEM((arrived.shape[0], INFO_ROWS, C), bf16),
            pltpu.VMEM((8, C), jnp.int32),
            pltpu.SemaphoreType.DMA((LEAD // 2,)),
        ],
        compiler_params=params(),
        name="block_order",
    )(arrived, *ready)


def edge_rows(wide, column):
    return wide[pl.ds(column, wide.shape[0] // COLS, stride=COLS), :]


EDGE_ROWS = (LEAD + 2 * OWN) * ROWS


def put_edges(wide, start, left_ref, right_ref):
    count = wide.shape[0] // COLS
    for c in range(2):
        at = pl.ds(c * EDGE_ROWS + start, count)
        left_ref[at] = edge_rows(wide, c).astype(bf16)
        right_ref[at] = edge_rows(wide, COLS - 2 + c).astype(bf16)


def place_kernel(order_ref, arrived_ref, frames_ref, left_ref, right_ref, wide, sems):
    copies = [
        pltpu.make_async_copy(
            block_at(arrived_ref, order_ref[0, k]),
            frames_ref.at[pl.ds(k * 2 * POS, 2 * POS)],
            sems.at[k],
        )
        for k in range(OWN)
    ]
    for copy in copies:
        copy.start()
    for k in range(OWN):
        copies[k].wait()
        wide[k % 2] = frames_ref[k * 2 * POS : (k + 1) * 2 * POS].astype(f32)
        put_edges(wide.at[k % 2], (LEAD + 2 * k) * ROWS, left_ref, right_ref)


def edge_shape(dtype):
    return jax.ShapeDtypeStruct((2 * EDGE_ROWS, C), dtype)


def place_blocks(order, arrived):
    edge = edge_shape(bf16)
    return pl.pallas_call(
        place_kernel,
        out_shape=(jax.ShapeDtypeStruct((2 * OWN * POS, C), bf16), edge, edge),
        in_specs=[smem(), hbm_only()],
        out_specs=(vmem(), vmem(), vmem()),
        scratch_shapes=[
            pltpu.VMEM((2, 2 * POS, C), f32),
            pltpu.SemaphoreType.DMA((OWN,)),
        ],
        compiler_params=params(),
        name="place_blocks",
    )(order, arrived)


def lead_kernel(lead_ref, left_in, right_in, left_ref, right_ref, wide):
    wide[...] = lead_ref[...].astype(f32)
    left_ref[...] = left_in[...]
    right_ref[...] = right_in[...]
    put_edges(wide, 0, left_ref, right_ref)


def lead_edges(lead, left, right):
    edge = edge_shape(bf16)
    return pl.pallas_call(
        lead_kernel,
        out_shape=(edge, edge),
        in_specs=[vmem()] * 3,
        out_specs=(vmem(), vmem()),
        scratch_shapes=[pltpu.VMEM((LEAD * POS, C), f32)],
        compiler_params=params(),
        name="lead_edges",
    )(lead, left, right)


def join_kernel(first_ref, second_ref, first_out, second_out, token_out):
    token_out[...] = jnp.zeros_like(token_out)
    for weight_ref, joined in ((first_ref, first_out), (second_ref, second_out)):
        for j in range(3):
            for i in range(3):
                for lag in range(3):
                    at = (3 * j + i) * C
                    joined[at : at + C, lag * C : (lag + 1) * C] = weight_ref[2 - lag, i, j]


def join_weights(first, second):
    joined = jax.ShapeDtypeStruct((9 * C, 3 * C), bf16)
    return pl.pallas_call(
        join_kernel,
        out_shape=(joined, joined, jax.ShapeDtypeStruct((8, C), f32)),
        in_specs=[vmem()] * 2,
        out_specs=(vmem(),) * 3,
        compiler_params=params(),
        name="join_weights",
    )(first, second)


def conv_chunk(valid_ref, start, count, wide, taps, joined, carry):
    for at in range(count * ROWS):
        q, r = at // ROWS, at % ROWS + 1
        base = at * PITCH + 8
        for j in range(3):
            taps[j, q, r] = wide[base + j - 1 : base + j - 1 + COLS].astype(bf16)
    windows = jnp.concatenate(
        [
            taps[j, 0:count, i : i + ROWS].reshape(count * POS, C)
            for j in range(3)
            for i in range(3)
        ],
        axis=1,
    )
    product = jnp.dot(windows, joined[...], preferred_element_type=f32)

    def part(q, lag):
        return product[q * POS : (q + 1) * POS, lag * C : (lag + 1) * C]

    totals = []
    for q in range(count):
        one = part(q - 1, 1) if q >= 1 else carry[0]
        two = part(q - 2, 2) if q >= 2 else carry[1 + q]
        totals.append(
            part(q, 0) + valid_ref[0, start + q] * one + valid_ref[1, start + q] * two
        )
    carry[0] = part(count - 1, 1)
    carry[1] = part(count - 2, 2)
    carry[2] = part(count - 1, 2)
    return totals


def conv_scratch():
    return [
        pltpu.VMEM((UNROLL, CHUNK * ROWS * PITCH + 8, C), f32),
        pltpu.VMEM((UNROLL, 3, CHUNK, ROWS + 2, COLS, C), bf16),
        pltpu.VMEM((3, POS, C), f32),
    ]


def conv_setup(taps, carry):
    carry[...] = jnp.zeros_like(carry)
    for u in range(UNROLL):
        for j in range(3):
            for edge in (0, ROWS + 1):
                taps[u, j, :, edge] = jnp.zeros((CHUNK, COLS, C), bf16)


def put_column(wide, at, column):
    wide[pl.ds(at, column.shape[0], stride=PITCH), :] = column


def over_chunks(chunk_step):
    def step(trip, done):
        for u in range(UNROLL):
            chunk_step(u, (trip * UNROLL + u) * CHUNK)
        return done

    lax.fori_loop(0, 2 * OWN // CHUNK // UNROLL, step, 0)


def group_total(entries):
    lane = lax.broadcasted_iota(jnp.int32, entries.shape, 1)
    for bit in (1, 2):
        up = pltpu.roll(entries, C - bit, 1)
        down = pltpu.roll(entries, bit, 1)
        entries = entries + jnp.where((lane & bit) == 0, up, down)
    return entries


def precise_dot(a, b):
    return jnp.dot(a, b, precision=lax.Precision.HIGHEST, preferred_element_type=f32)


INNER = ROWS * (COLS - 2)


def hidden_kernel(
    valid_ref, lead_ref, frames_ref, joined, hidden_ref, means_ref, spreads_ref,
    wide, taps, carry,
):
    conv_setup(taps, carry)
    none = jnp.zeros((CHUNK * ROWS, C), f32)
    for u in range(UNROLL):
        put_column(wide.at[u], 7, none)
        put_column(wide.at[u], 8 + COLS, none)
    means_ref[...] = jnp.zeros_like(means_ref)
    spreads_ref[...] = jnp.zeros_like(spreads_ref)
    column = lax.broadcasted_iota(jnp.int32, (POS, C), 0) % COLS
    inner = (column > 0) & (column < COLS - 1)

    def chunk_step(u, start, count, source, at):
        for row in range(count * ROWS):
            here = source[pl.ds(pl.multiple_of(at + row * COLS, COLS), COLS)]
            wide[u, row * PITCH + 8 : row * PITCH + 8 + COLS] = here.astype(f32)
        totals = conv_chunk(valid_ref, start, count, wide.at[u], taps.at[u], joined, carry)
        for q in range(count):
            frame = start + q
            own = totals[q]
            hidden_ref[frame] = own
            mean = jnp.sum(jnp.where(inner, own, 0.0), axis=0, keepdims=True) / INNER
            centred = jnp.where(inner, own - mean, 0.0)
            means_ref[pl.ds(frame, 1), :] = mean
            spreads_ref[pl.ds(frame, 1), :] = jnp.sum(centred * centred, axis=0, keepdims=True)

    chunk_step(0, 0, LEAD, lead_ref, 0)
    over_chunks(lambda u, at: chunk_step(u, LEAD + at, CHUNK, frames_ref, at * POS))


def first_layer(valid, lead, frames, joined):
    length = LEAD + 2 * OWN
    sums = jax.ShapeDtypeStruct((2 * HALF, C), f32)
    return pl.pallas_call(
        hidden_kernel,
        out_shape=(jax.ShapeDtypeStruct((length, POS, C), f32), sums, sums),
        in_specs=[smem()] + [vmem()] * 3,
        out_specs=(vmem(),) * 3,
        scratch_shapes=conv_scratch(),
        compiler_params=params(),
        cost_estimate=pl.CostEstimate(
            flops=2 * length * POS * 27 * C * C, bytes_accessed=4 * MIB, transcendentals=0
        ),
        name="first_layer",
    )(valid, lead, frames, joined)


def edge_kernel(
    valid_ref, own_l, own_r, halo_l, halo_r, joined, means_ref, spreads_ref,
    edges_ref, stats_ref, means, spreads,
):
    row = lax.broadcasted_iota(jnp.int32, (EDGE_ROWS, C), 0) % ROWS
    length = EDGE_ROWS // ROWS

    def rows_of(ref, c):
        column = ref[c * EDGE_ROWS : (c + 1) * EDGE_ROWS].astype(f32)
        above = jnp.where(row == 0, 0.0, pltpu.roll(column, 1, 0))
        below = jnp.where(row == ROWS - 1, 0.0, pltpu.roll(column, EDGE_ROWS - 1, 0))
        return [piece.astype(bf16) for piece in (above, column, below)]

    for side, refs in enumerate(((halo_l, own_l), (own_r, halo_r))):
        columns = [rows_of(ref, c) for ref in refs for c in range(2)]
        for k in range(2):
            windows = jnp.concatenate(sum(columns[k : k + 3], []), axis=1)
            product = jnp.dot(windows, joined[...], preferred_element_type=f32)

            def part(frame, lag):
                rows = slice(frame * ROWS, (frame + 1) * ROWS)
                return product[rows, lag * C : (lag + 1) * C]

            at = 2 * side + k
            edges_ref[at, 0 : 2 * ROWS] = jnp.zeros((2 * ROWS, C), f32)
            for frame in range(2, length):
                edges_ref[at, frame * ROWS : (frame + 1) * ROWS] = (
                    part(frame, 0)
                    + valid_ref[0, frame] * part(frame - 1, 1)
                    + valid_ref[1, frame] * part(frame - 2, 2)
                )

    means[...] = jnp.zeros_like(means)
    spreads[...] = jnp.zeros_like(spreads)
    outer = [edges_ref[at].reshape(length, ROWS, C) for at in (1, 2)]
    mean = jnp.sum(outer[0] + outer[1], axis=1, keepdims=True) / (2 * ROWS)
    apart = [(entries - mean) * (entries - mean) for entries in outer]
    means[0:length] = mean.reshape(length, C)
    spreads[0:length] = jnp.sum(apart[0] + apart[1], axis=1)
    off = means[...] - means_ref[...]
    local = means_ref[...] + off * (2 * ROWS / POS)
    spread = spreads_ref[...] + spreads[...] + off * off * (INNER * 2 * ROWS / POS)

    mean = group_total(local) / 4
    off = local - mean
    spread = group_total(spread + POS * off * off)
    channel = lax.broadcasted_iota(jnp.int32, (C, C), 0)
    lane = lax.broadcasted_iota(jnp.int32, (C, C), 1)
    packed = jnp.zeros((HALF, C), f32)
    for q, piece in enumerate((mean[:HALF], spread[:HALF], mean[HALF:], spread[HALF:])):
        picks = (channel == 4 * (lane - GROUPS * q)) & (lane // GROUPS == q)
        packed = packed + precise_dot(piece, picks.astype(f32))
    for peer in range(stats_ref.shape[0]):
        stats_ref[peer] = packed


def finish_hidden(valid, own_l, own_r, halo_l, halo_r, joined, means, spreads, tiles):
    return pl.pallas_call(
        edge_kernel,
        out_shape=(
            jax.ShapeDtypeStruct((4, EDGE_ROWS, C), f32),
            jax.ShapeDtypeStruct((tiles, HALF, C), f32),
        ),
        in_specs=[smem()] + [vmem()] * 7,
        out_specs=(vmem(),) * 2,
        scratch_shapes=[pltpu.VMEM((2 * HALF, C), f32), pltpu.VMEM((2 * HALF, C), f32)],
        compiler_params=params(),
        name="finish_hidden",
    )(valid, own_l, own_r, halo_l, halo_r, joined, means, spreads)


def combine_stats(stats_ref, gain_ref, means, scales):
    tiles = stats_ref.shape[0]
    here = POS * (C // GROUPS)
    lane = lax.broadcasted_iota(jnp.int32, (HALF, C), 1)
    is_mean = (lane // GROUPS) % 2 == 0
    total = stats_ref[0]
    for peer in range(1, tiles):
        total = total + stats_ref[peer]
    mean = total / tiles
    apart = jnp.zeros((HALF, C), f32)
    for peer in range(tiles):
        off = stats_ref[peer] - mean
        apart = apart + off * off
    apart = jnp.where(is_mean, apart, 0.0)
    variance = (total + here * pltpu.roll(apart, GROUPS, 1)) / (here * tiles)
    packed = jnp.where(is_mean, mean, lax.rsqrt(jnp.where(is_mean, 1.0, variance) + EPSILON))
    channel = lax.broadcasted_iota(jnp.int32, (C, C), 1)
    source = lax.broadcasted_iota(jnp.int32, (C, C), 0)
    for q in range(4):
        picks = (source == channel // (C // GROUPS) + GROUPS * q).astype(f32)
        target = scales if q % 2 else means
        half = pl.ds((q // 2) * HALF, HALF)
        target[half, :] = precise_dot(packed, picks)
    scales[...] = scales[...] * gain_ref[...]


def silu(v):
    return v * (1.0 / (1.0 + jnp.exp(-v)))


def output_kernel(
    valid_ref, hidden_ref, edges_ref, stats_ref, frames_ref,
    gain_ref, norm_bias_ref, joined, bias_ref, out_ref,
    wide, taps, carry, means, scales, halo,
):
    conv_setup(taps, carry)
    combine_stats(stats_ref, gain_ref, means, scales)
    has_left = valid_ref[2, 0]
    has_right = valid_ref[2, 1]

    def norm(hidden, frame):
        centred = hidden - means[pl.ds(frame, 1), :]
        return silu(centred * scales[pl.ds(frame, 1), :] + norm_bias_ref[...])

    def chunk_step(u, start, count):
        for q in range(count):
            frame = start + q
            active = norm(hidden_ref[frame], frame)
            for r in range(ROWS):
                at = (q * ROWS + r) * PITCH + 8
                wide[u, at : at + COLS] = active[r * COLS : (r + 1) * COLS]
            at = pl.ds(pl.multiple_of(frame * ROWS, ROWS), ROWS)
            for k, inside in enumerate((has_left, 1.0, 1.0, has_right)):
                halo[u, k, q * ROWS : (q + 1) * ROWS] = norm(edges_ref[k, at], frame) * inside
        for k, column in enumerate((7, 8, 7 + COLS, 8 + COLS)):
            put_column(wide.at[u], column, halo[u, k, 0 : count * ROWS])
        return conv_chunk(valid_ref, start, count, wide.at[u], taps.at[u], joined, carry)

    def own_chunk(u, start):
        totals = chunk_step(u, LEAD + start, CHUNK)
        for q in range(CHUNK):
            rows = pl.ds(pl.multiple_of((start + q) * POS, POS), POS)
            total = frames_ref[rows].astype(f32) + (totals[q] + bias_ref[...])
            out_ref[rows] = total.astype(bf16)

    chunk_step(0, LEAD - 2, 2)
    over_chunks(own_chunk)


def second_layer(valid, hidden, edges, stats, frames, gain, norm_bias, weight, bias):
    return pl.pallas_call(
        output_kernel,
        out_shape=jax.ShapeDtypeStruct(frames.shape, bf16),
        in_specs=[smem()] + [vmem()] * 8,
        out_specs=vmem(),
        scratch_shapes=conv_scratch()
        + [
            pltpu.VMEM((2 * HALF, C), f32),
            pltpu.VMEM((2 * HALF, C), f32),
            pltpu.VMEM((UNROLL, 4, CHUNK * ROWS, C), f32),
        ],
        compiler_params=params(),
        name="second_layer",
    )(valid, hidden, edges, stats, frames, gain, norm_bias, weight, bias)


def lag_masks(clip_frames, first_frame, length):
    clip_ends = jnp.cumsum(clip_frames)

    def clip_of(frames):
        ids = jnp.sum((frames[:, None] >= clip_ends[None, :]).astype(jnp.int32), axis=1)
        return jnp.where(frames < 0, -1, ids)

    frames = first_frame + jnp.arange(length, dtype=jnp.int32)
    here = clip_of(frames)
    return jnp.stack([clip_of(frames - lag) == here for lag in (1, 2)])


def swap_edges(left, right):
    count = lax.axis_size("tile")
    from_left = lax.ppermute(right, "tile", [(i, i + 1) for i in range(count - 1)])
    from_right = lax.ppermute(left, "tile", [(i + 1, i) for i in range(count - 1)])
    return from_left, from_right


def shards(
    video, slot_block, clip_frames, conv1_weight, norm_gain, norm_bias, conv2_weight, conv2_bias
):
    owners = lax.axis_size("tm")
    tiles = lax.axis_size("tile")
    position = lax.axis_index("tm")
    tile = lax.axis_index("tile")
    length = 2 * OWN

    outgoing = send_blocks(slot_block, video, owners)
    arrived = lax.all_to_all(outgoing, "tm", split_axis=0, concat_axis=0, tiled=True)

    inside = jnp.stack([tile > 0, tile < tiles - 1] + [tile < 0] * (length + LEAD - 2))
    valid = jnp.concatenate(
        [lag_masks(clip_frames, position * length - LEAD, length + LEAD), inside[None]]
    ).astype(f32)

    weight1, weight2, token = join_weights(conv1_weight, conv2_weight)
    order, tail = block_order(arrived, (valid, token))
    lead = lax.ppermute(tail, "tm", [(i, i + 1) for i in range(owners - 1)])
    frames, left, right = place_blocks(order, arrived)
    left, right = lead_edges(lead, left, right)
    from_left, from_right = swap_edges(left, right)
    hidden, means, spreads = first_layer(valid, lead, frames, weight1)
    edges, stats = finish_hidden(
        valid, left, right, from_left, from_right, weight1, means, spreads, tiles
    )
    stats = lax.all_to_all(stats, "tile", split_axis=0, concat_axis=0, tiled=True)
    encoded = second_layer(
        valid, hidden, edges, stats, frames, norm_gain[None], norm_bias[None],
        weight2, conv2_bias[None],
    )
    return encoded.reshape((length,) + video.shape[2:])


def solution(mesh):
    placed = (P("tm", None, None, "tile", None), P("tm"), P(), P(), P(), P(), P(), P())
    return jax.shard_map(
        shards, mesh=mesh, in_specs=placed, out_specs=P("tm", None, "tile", None), check_vma=False
    )
```

```python
import functools

import jax
import jax.numpy as jnp
from jax import lax
from jax.experimental import pallas as pl
from jax.experimental.pallas import tpu as pltpu
from jax.sharding import PartitionSpec as P

GROUPS = 32
OWN = 16
CAP = 2
C = 128
ROWS = 8
COLS = 16
POS = ROWS * COLS
LEAD = 4
CHUNK = 8
EPSILON = 1e-06
HALF = 24
PITCH = 24
UNROLL = 4
PAIR_ROWS = CAP * 2 * POS
INFO_ROWS = 16
MIB = 1024 * 1024

f32 = jnp.float32
bf16 = jnp.bfloat16


def vmem():
    return pl.BlockSpec(memory_space=pltpu.VMEM)


def smem():
    return pl.BlockSpec(memory_space=pltpu.SMEM)


def hbm():
    return pl.BlockSpec(memory_space=pl.ANY)


def params(mib=16):
    return pltpu.CompilerParams(vmem_limit_bytes=mib * MIB)


def hbm_only():
    return pl.BlockSpec(memory_space=pltpu.HBM)


LOADS = 4


def send_kernel(
    slot_hbm, video_ref, out_ref, slot_ref, count, target, held, info, info_out, sems_in, sems_out
):
    slots = slot_ref.shape[0]
    owners = out_ref.shape[0]
    block_rows = PAIR_ROWS // CAP

    def load(part):
        at = pl.ds(part * (slots // LOADS), slots // LOADS)
        return pltpu.make_async_copy(video_ref.at[at], held.at[at], sems_in.at[part])

    def store(slot, owner, rank):
        rows = pl.ds(pl.multiple_of(rank * block_rows, block_rows), block_rows)
        return pltpu.make_async_copy(
            held.at[slot], out_ref.at[owner, rows], sems_out.at[slot]
        )

    to_scalars = pltpu.make_async_copy(slot_hbm, slot_ref, sems_in.at[LOADS])
    to_scalars.start()
    for part in range(LOADS):
        load(part).start()
    for owner in range(owners + 1):
        count[owner] = 0
    info[...] = jnp.zeros_like(info)
    lane = lax.broadcasted_iota(jnp.int32, info.shape[1:], 1)
    to_scalars.wait()
    for slot in range(slots):
        block = slot_ref[slot]
        owner = jnp.where(block >= 0, block >> 4, owners)
        rank = count[owner]
        count[owner] = rank + 1
        target[slot] = rank
        mark = jnp.where(lane == (block & (OWN - 1)), (rank + 1).astype(f32), 0.0)
        info[owner] = info[owner] + mark
    for owner in range(owners):
        info_out[owner] = jnp.concatenate([info[owner]] * 2, axis=0).astype(bf16)
    notes = pltpu.make_async_copy(
        info_out, out_ref.at[:, pl.ds(PAIR_ROWS, INFO_ROWS)], sems_out.at[slots]
    )
    notes.start()
    for slot in range(slots):
        if slot % (slots // LOADS) == 0:
            load(slot // (slots // LOADS)).wait()

        @pl.when(slot_ref[slot] >= 0)
        def _():
            store(slot, slot_ref[slot] >> 4, target[slot]).start()

    for slot in range(slots):

        @pl.when(slot_ref[slot] >= 0)
        def _():
            store(slot, 0, 0).wait()

    notes.wait()


def send_blocks(slot_block, video, owners):
    slots = video.shape[0]
    return pl.pallas_call(
        send_kernel,
        out_shape=jax.ShapeDtypeStruct((owners, PAIR_ROWS + INFO_ROWS, C), video.dtype),
        in_specs=[hbm_only(), hbm_only()],
        out_specs=hbm_only(),
        scratch_shapes=[
            pltpu.SMEM((slots,), jnp.int32),
            pltpu.SMEM((owners + 1,), jnp.int32),
            pltpu.SMEM((slots,), jnp.int32),
            pltpu.VMEM((slots, PAIR_ROWS // CAP, C), bf16),
            pltpu.VMEM((owners + 1, 8, C), f32),
            pltpu.VMEM((owners, INFO_ROWS, C), bf16),
            pltpu.SemaphoreType.DMA((LOADS + 1,)),
            pltpu.SemaphoreType.DMA((slots + 1,)),
        ],
        compiler_params=params(62),
        name="send_blocks",
    )(slot_block, video.reshape(slots, PAIR_ROWS // CAP, C))


def order_kernel(arrived_ref, *refs):
    order_ref, tail_ref, picks, sem = refs[-4:]
    total = jnp.zeros((INFO_ROWS, C), f32)
    for source in range(arrived_ref.shape[0]):
        rank = arrived_ref[source, PAIR_ROWS:].astype(f32)
        total = total + jnp.where(rank > 0.0, rank + (CAP * source - 1.0), 0.0)
    picks[...] = total[0:8].astype(jnp.int32)
    to_scalars = pltpu.make_async_copy(picks.at[pl.ds(0, 1)], order_ref, sem)
    to_scalars.start()
    to_scalars.wait()
    for k in range(LEAD // 2):
        block = block_at(arrived_ref, order_ref[0, OWN - LEAD // 2 + k])
        tail_ref[k * 2 * POS : (k + 1) * 2 * POS] = block


def block_at(arrived_ref, arrival):
    block_rows = PAIR_ROWS // CAP
    rows = pl.ds(pl.multiple_of((arrival & 1) * block_rows, block_rows), block_rows)
    return arrived_ref[arrival >> 1, rows]


def block_order(arrived, ready):
    return pl.pallas_call(
        order_kernel,
        out_shape=(
            jax.ShapeDtypeStruct((1, C), jnp.int32),
            jax.ShapeDtypeStruct((LEAD * POS, C), bf16),
        ),
        in_specs=[vmem()] + [hbm()] * len(ready),
        out_specs=(smem(), vmem()),
        scratch_shapes=[pltpu.VMEM((8, C), jnp.int32), pltpu.SemaphoreType.DMA],
        compiler_params=params(),
        name="block_order",
    )(arrived, *ready)


def edge_rows(wide, column):
    return wide[pl.ds(column, wide.shape[0] // COLS, stride=COLS), :]


EDGE_ROWS = (LEAD + 2 * OWN) * ROWS


def put_edges(wide, start, left_ref, right_ref):
    count = wide.shape[0] // COLS
    for c in range(2):
        at = pl.ds(c * EDGE_ROWS + start, count)
        left_ref[at] = edge_rows(wide, c).astype(bf16)
        right_ref[at] = edge_rows(wide, COLS - 2 + c).astype(bf16)


def place_kernel(order_ref, arrived_ref, frames_ref, left_ref, right_ref, wide):
    for k in range(OWN):
        block = block_at(arrived_ref, order_ref[0, k])
        frames_ref[k * 2 * POS : (k + 1) * 2 * POS] = block
        wide[k % 2] = block.astype(f32)
        put_edges(wide.at[k % 2], (LEAD + 2 * k) * ROWS, left_ref, right_ref)


def edge_shape(dtype):
    return jax.ShapeDtypeStruct((2 * EDGE_ROWS, C), dtype)


def place_blocks(order, arrived):
    edge = edge_shape(bf16)
    return pl.pallas_call(
        place_kernel,
        out_shape=(jax.ShapeDtypeStruct((2 * OWN * POS, C), bf16), edge, edge),
        in_specs=[smem(), vmem()],
        out_specs=(vmem(), vmem(), vmem()),
        scratch_shapes=[pltpu.VMEM((2, 2 * POS, C), f32)],
        compiler_params=params(),
        name="place_blocks",
    )(order, arrived)


def lead_kernel(lead_ref, left_in, right_in, left_ref, right_ref, wide):
    wide[...] = lead_ref[...].astype(f32)
    left_ref[...] = left_in[...]
    right_ref[...] = right_in[...]
    put_edges(wide, 0, left_ref, right_ref)


def lead_edges(lead, left, right):
    edge = edge_shape(bf16)
    return pl.pallas_call(
        lead_kernel,
        out_shape=(edge, edge),
        in_specs=[vmem()] * 3,
        out_specs=(vmem(), vmem()),
        scratch_shapes=[pltpu.VMEM((LEAD * POS, C), f32)],
        compiler_params=params(),
        name="lead_edges",
    )(lead, left, right)


def join_kernel(first_ref, second_ref, edge_out, first_out, second_out, token_out):
    token_out[...] = jnp.zeros_like(token_out)
    for j in range(3):
        for lag in range(3):
            for i in range(3):
                at = (3 * j + i) * C
                edge_out[at : at + C, lag * C : (lag + 1) * C] = first_ref[2 - lag, i, j]
            for weight_ref, joined in ((first_ref, first_out), (second_ref, second_out)):
                for i in range(4):
                    for parity in range(2):
                        at = (4 * j + i) * C
                        lane = (3 * parity + lag) * C
                        inside = 0 <= i - parity <= 2
                        joined[at : at + C, lane : lane + C] = (
                            weight_ref[2 - lag, i - parity, j] if inside else jnp.zeros((C, C), bf16)
                        )


def join_weights(first, second):
    edge = jax.ShapeDtypeStruct((9 * C, 3 * C), bf16)
    joined = jax.ShapeDtypeStruct((12 * C, 6 * C), bf16)
    return pl.pallas_call(
        join_kernel,
        out_shape=(edge, joined, joined, jax.ShapeDtypeStruct((8, C), f32)),
        in_specs=[vmem()] * 2,
        out_specs=(vmem(),) * 4,
        compiler_params=params(),
        name="join_weights",
    )(first, second)


def conv_chunk(valid_ref, start, count, wide, taps, joined, carry):
    for at in range(count * ROWS):
        q, r = at // ROWS, at % ROWS + 1
        base = at * PITCH + 8
        for j in range(3):
            taps[j, q, r] = wide[base + j - 1 : base + j - 1 + COLS].astype(bf16)
    windows = jnp.concatenate(
        [
            jnp.concatenate(
                [taps[j, q, i + 2 * p] for q in range(count) for p in range(ROWS // 2)], axis=0
            )
            for j in range(3)
            for i in range(4)
        ],
        axis=1,
    )
    product = jnp.dot(windows, joined[...], preferred_element_type=f32)

    def part(q, lag):
        rows = []
        for r in range(ROWS):
            at = (q * (ROWS // 2) + r // 2) * COLS
            lane = (3 * (r % 2) + lag) * C
            rows.append(product[at : at + COLS, lane : lane + C])
        return jnp.concatenate(rows, axis=0)

    totals = []
    for q in range(count):
        one = part(q - 1, 1) if q >= 1 else carry[0]
        two = part(q - 2, 2) if q >= 2 else carry[1 + q]
        totals.append(
            part(q, 0) + valid_ref[0, start + q] * one + valid_ref[1, start + q] * two
        )
    carry[0] = part(count - 1, 1)
    carry[1] = part(count - 2, 2)
    carry[2] = part(count - 1, 2)
    return totals


def conv_scratch():
    return [
        pltpu.VMEM((UNROLL, CHUNK * ROWS * PITCH + 8, C), f32),
        pltpu.VMEM((UNROLL, 3, CHUNK, ROWS + 2, COLS, C), bf16),
        pltpu.VMEM((3, POS, C), f32),
    ]


def conv_setup(taps, carry):
    carry[...] = jnp.zeros_like(carry)
    for u in range(UNROLL):
        for j in range(3):
            for edge in (0, ROWS + 1):
                taps[u, j, :, edge] = jnp.zeros((CHUNK, COLS, C), bf16)


def put_column(wide, at, column):
    wide[pl.ds(at, column.shape[0], stride=PITCH), :] = column


def over_chunks(chunk_step):
    def step(trip, done):
        for u in range(UNROLL):
            chunk_step(u, (trip * UNROLL + u) * CHUNK)
        return done

    lax.fori_loop(0, 2 * OWN // CHUNK // UNROLL, step, 0)


def group_total(entries):
    lane = lax.broadcasted_iota(jnp.int32, entries.shape, 1)
    for bit in (1, 2):
        up = pltpu.roll(entries, C - bit, 1)
        down = pltpu.roll(entries, bit, 1)
        entries = entries + jnp.where((lane & bit) == 0, up, down)
    return entries


def pick_columns(entries, picks):
    count = entries.shape[0]
    parts = []
    for _ in range(3):
        parts.append(entries.astype(bf16))
        entries = entries - parts[-1].astype(f32)
    picked = jnp.dot(
        jnp.concatenate(parts, axis=0), picks.astype(bf16), preferred_element_type=f32
    )
    return picked[0:count] + picked[count : 2 * count] + picked[2 * count :]


INNER = ROWS * (COLS - 2)


def hidden_kernel(
    valid_ref, lead_ref, frames_ref, joined, hidden_ref, means_ref, spreads_ref,
    wide, taps, carry,
):
    conv_setup(taps, carry)
    none = jnp.zeros((CHUNK * ROWS, C), f32)
    for u in range(UNROLL):
        put_column(wide.at[u], 7, none)
        put_column(wide.at[u], 8 + COLS, none)
    means_ref[...] = jnp.zeros_like(means_ref)
    spreads_ref[...] = jnp.zeros_like(spreads_ref)
    column = lax.broadcasted_iota(jnp.int32, (POS, C), 0) % COLS
    inner = (column > 0) & (column < COLS - 1)

    def chunk_step(u, start, count, source, at):
        for row in range(count * ROWS):
            here = source[pl.ds(pl.multiple_of(at + row * COLS, COLS), COLS)]
            wide[u, row * PITCH + 8 : row * PITCH + 8 + COLS] = here.astype(f32)
        totals = conv_chunk(valid_ref, start, count, wide.at[u], taps.at[u], joined, carry)
        for q in range(count):
            frame = start + q
            own = totals[q]
            hidden_ref[frame] = own
            mean = jnp.sum(jnp.where(inner, own, 0.0), axis=0, keepdims=True) / INNER
            centred = jnp.where(inner, own - mean, 0.0)
            means_ref[pl.ds(frame, 1), :] = mean
            spreads_ref[pl.ds(frame, 1), :] = jnp.sum(centred * centred, axis=0, keepdims=True)

    chunk_step(0, 0, LEAD, lead_ref, 0)
    over_chunks(lambda u, at: chunk_step(u, LEAD + at, CHUNK, frames_ref, at * POS))


def first_layer(valid, lead, frames, joined):
    length = LEAD + 2 * OWN
    sums = jax.ShapeDtypeStruct((2 * HALF, C), f32)
    return pl.pallas_call(
        hidden_kernel,
        out_shape=(jax.ShapeDtypeStruct((length, POS, C), f32), sums, sums),
        in_specs=[smem()] + [vmem()] * 3,
        out_specs=(vmem(),) * 3,
        scratch_shapes=conv_scratch(),
        compiler_params=params(),
        cost_estimate=pl.CostEstimate(
            flops=2 * length * POS * 27 * C * C, bytes_accessed=4 * MIB, transcendentals=0
        ),
        name="first_layer",
    )(valid, lead, frames, joined)


def edge_kernel(
    valid_ref, own_l, own_r, halo_l, halo_r, joined, means_ref, spreads_ref,
    edges_ref, stats_ref, means, spreads,
):
    row = lax.broadcasted_iota(jnp.int32, (EDGE_ROWS, C), 0) % ROWS
    length = EDGE_ROWS // ROWS

    def rows_of(ref, c):
        column = ref[c * EDGE_ROWS : (c + 1) * EDGE_ROWS].astype(f32)
        above = jnp.where(row == 0, 0.0, pltpu.roll(column, 1, 0))
        below = jnp.where(row == ROWS - 1, 0.0, pltpu.roll(column, EDGE_ROWS - 1, 0))
        return [piece.astype(bf16) for piece in (above, column, below)]

    for side, refs in enumerate(((halo_l, own_l), (own_r, halo_r))):
        columns = [rows_of(ref, c) for ref in refs for c in range(2)]
        for k in range(2):
            windows = jnp.concatenate(sum(columns[k : k + 3], []), axis=1)
            product = jnp.dot(windows, joined[...], preferred_element_type=f32)

            def part(frame, lag):
                rows = slice(frame * ROWS, (frame + 1) * ROWS)
                return product[rows, lag * C : (lag + 1) * C]

            at = 2 * side + k
            edges_ref[at, 0 : 2 * ROWS] = jnp.zeros((2 * ROWS, C), f32)
            for frame in range(2, length):
                edges_ref[at, frame * ROWS : (frame + 1) * ROWS] = (
                    part(frame, 0)
                    + valid_ref[0, frame] * part(frame - 1, 1)
                    + valid_ref[1, frame] * part(frame - 2, 2)
                )

    means[...] = jnp.zeros_like(means)
    spreads[...] = jnp.zeros_like(spreads)
    outer = [edges_ref[at].reshape(length, ROWS, C) for at in (1, 2)]
    mean = jnp.sum(outer[0] + outer[1], axis=1, keepdims=True) / (2 * ROWS)
    apart = [(entries - mean) * (entries - mean) for entries in outer]
    means[0:length] = mean.reshape(length, C)
    spreads[0:length] = jnp.sum(apart[0] + apart[1], axis=1)
    off = means[...] - means_ref[...]
    local = means_ref[...] + off * (2 * ROWS / POS)
    spread = spreads_ref[...] + spreads[...] + off * off * (INNER * 2 * ROWS / POS)

    mean = group_total(local) / 4
    off = local - mean
    spread = group_total(spread + POS * off * off)
    pieces = (mean[:HALF], spread[:HALF], mean[HALF:], spread[HALF:])
    channel = lax.broadcasted_iota(jnp.int32, (4 * C, C), 0)
    lane = lax.broadcasted_iota(jnp.int32, (4 * C, C), 1)
    picks = channel == C * (lane // GROUPS) + (C // GROUPS) * (lane % GROUPS)
    packed = pick_columns(jnp.concatenate(pieces, axis=1), picks.astype(f32))
    for peer in range(stats_ref.shape[0]):
        stats_ref[peer] = packed


def finish_hidden(valid, own_l, own_r, halo_l, halo_r, joined, means, spreads, tiles):
    return pl.pallas_call(
        edge_kernel,
        out_shape=(
            jax.ShapeDtypeStruct((4, EDGE_ROWS, C), f32),
            jax.ShapeDtypeStruct((tiles, HALF, C), f32),
        ),
        in_specs=[smem()] + [vmem()] * 7,
        out_specs=(vmem(),) * 2,
        scratch_shapes=[pltpu.VMEM((2 * HALF, C), f32), pltpu.VMEM((2 * HALF, C), f32)],
        compiler_params=params(),
        name="finish_hidden",
    )(valid, own_l, own_r, halo_l, halo_r, joined, means, spreads)


def combine_stats(stats_ref, gain_ref, means, scales):
    tiles = stats_ref.shape[0]
    here = POS * (C // GROUPS)
    lane = lax.broadcasted_iota(jnp.int32, (HALF, C), 1)
    is_mean = (lane // GROUPS) % 2 == 0
    total = stats_ref[0]
    for peer in range(1, tiles):
        total = total + stats_ref[peer]
    mean = total / tiles
    apart = jnp.zeros((HALF, C), f32)
    for peer in range(tiles):
        off = stats_ref[peer] - mean
        apart = apart + off * off
    apart = jnp.where(is_mean, apart, 0.0)
    variance = (total + here * pltpu.roll(apart, GROUPS, 1)) / (here * tiles)
    packed = jnp.where(is_mean, mean, lax.rsqrt(jnp.where(is_mean, 1.0, variance) + EPSILON))
    source = lax.broadcasted_iota(jnp.int32, (C, 4 * C), 0)
    column = lax.broadcasted_iota(jnp.int32, (C, 4 * C), 1)
    picks = source == GROUPS * (column // C) + (column % C) // (C // GROUPS)
    spread_out = pick_columns(packed, picks.astype(f32))
    means[0:HALF] = spread_out[:, 0:C]
    scales[0:HALF] = spread_out[:, C : 2 * C]
    means[HALF:] = spread_out[:, 2 * C : 3 * C]
    scales[HALF:] = spread_out[:, 3 * C :]
    scales[...] = scales[...] * gain_ref[...]


def silu(v):
    return v * (1.0 / (1.0 + jnp.exp(-v)))


def output_kernel(
    valid_ref, hidden_ref, edges_ref, stats_ref, frames_ref,
    gain_ref, norm_bias_ref, joined, bias_ref, out_ref,
    wide, taps, carry, means, scales, halo, staged, sems,
):
    conv_setup(taps, carry)
    combine_stats(stats_ref, gain_ref, means, scales)
    has_left = valid_ref[2, 0]
    has_right = valid_ref[2, 1]

    def norm(hidden, frame):
        centred = hidden - means[pl.ds(frame, 1), :]
        return silu(centred * scales[pl.ds(frame, 1), :] + norm_bias_ref[...])

    def chunk_step(u, start, count):
        for q in range(count):
            frame = start + q
            active = norm(hidden_ref[frame], frame)
            for r in range(ROWS):
                at = (q * ROWS + r) * PITCH + 8
                wide[u, at : at + COLS] = active[r * COLS : (r + 1) * COLS]
            at = pl.ds(pl.multiple_of(frame * ROWS, ROWS), ROWS)
            for k, inside in enumerate((has_left, 1.0, 1.0, has_right)):
                halo[u, k, q * ROWS : (q + 1) * ROWS] = norm(edges_ref[k, at], frame) * inside
        for k, column in enumerate((7, 8, 7 + COLS, 8 + COLS)):
            put_column(wide.at[u], column, halo[u, k, 0 : count * ROWS])
        return conv_chunk(valid_ref, start, count, wide.at[u], taps.at[u], joined, carry)

    def own_chunk(u, start):
        totals = chunk_step(u, LEAD + start, CHUNK)
        for q in range(CHUNK):
            rows = pl.ds(pl.multiple_of((start + q) * POS, POS), POS)
            total = frames_ref[rows].astype(f32) + (totals[q] + bias_ref[...])
            staged[rows] = total.astype(bf16)
        copy_out(start).start()

    def copy_out(start):
        rows = pl.ds(pl.multiple_of(start * POS, CHUNK * POS), CHUNK * POS)
        sem = sems.at[lax.div(jnp.int32(start), jnp.int32(CHUNK))]
        return pltpu.make_async_copy(staged.at[rows], out_ref.at[rows], sem)

    chunk_step(0, LEAD - 2, 2)
    over_chunks(own_chunk)
    for start in range(0, 2 * OWN, CHUNK):
        copy_out(start).wait()


def second_layer(valid, hidden, edges, stats, frames, gain, norm_bias, weight, bias):
    return pl.pallas_call(
        output_kernel,
        out_shape=jax.ShapeDtypeStruct(frames.shape, bf16),
        in_specs=[smem()] + [vmem()] * 8,
        out_specs=hbm_only(),
        scratch_shapes=conv_scratch()
        + [
            pltpu.VMEM((2 * HALF, C), f32),
            pltpu.VMEM((2 * HALF, C), f32),
            pltpu.VMEM((UNROLL, 4, CHUNK * ROWS, C), f32),
            pltpu.VMEM(frames.shape, bf16),
            pltpu.SemaphoreType.DMA((2 * OWN // CHUNK,)),
        ],
        compiler_params=params(),
        name="second_layer",
    )(valid, hidden, edges, stats, frames, gain, norm_bias, weight, bias)


def lag_masks(clip_frames, first_frame, length):
    clip_ends = jnp.cumsum(clip_frames)

    def clip_of(frames):
        ids = jnp.sum((frames[:, None] >= clip_ends[None, :]).astype(jnp.int32), axis=1)
        return jnp.where(frames < 0, -1, ids)

    frames = first_frame + jnp.arange(length, dtype=jnp.int32)
    here = clip_of(frames)
    return jnp.stack([clip_of(frames - lag) == here for lag in (1, 2)])


def swap_edges(left, right):
    count = lax.axis_size("tile")
    from_left = lax.ppermute(right, "tile", [(i, i + 1) for i in range(count - 1)])
    from_right = lax.ppermute(left, "tile", [(i + 1, i) for i in range(count - 1)])
    return from_left, from_right


def shards(
    video, slot_block, clip_frames, conv1_weight, norm_gain, norm_bias, conv2_weight, conv2_bias
):
    owners = lax.axis_size("tm")
    tiles = lax.axis_size("tile")
    position = lax.axis_index("tm")
    tile = lax.axis_index("tile")
    length = 2 * OWN

    outgoing = send_blocks(slot_block, video, owners)
    arrived = lax.all_to_all(outgoing, "tm", split_axis=0, concat_axis=0, tiled=True)

    inside = jnp.stack([tile > 0, tile < tiles - 1] + [tile < 0] * (length + LEAD - 2))
    valid = jnp.concatenate(
        [lag_masks(clip_frames, position * length - LEAD, length + LEAD), inside[None]]
    ).astype(f32)

    weight_edge, weight1, weight2, token = join_weights(conv1_weight, conv2_weight)
    order, tail = block_order(arrived, (valid, token))
    lead = lax.ppermute(tail, "tm", [(i, i + 1) for i in range(owners - 1)])
    frames, left, right = place_blocks(order, arrived)
    left, right = lead_edges(lead, left, right)
    from_left, from_right = swap_edges(left, right)
    hidden, means, spreads = first_layer(valid, lead, frames, weight1)
    edges, stats = finish_hidden(
        valid, left, right, from_left, from_right, weight_edge, means, spreads, tiles
    )
    stats = lax.all_to_all(stats, "tile", split_axis=0, concat_axis=0, tiled=True)
    encoded = second_layer(
        valid, hidden, edges, stats, frames, norm_gain[None], norm_bias[None],
        weight2, conv2_bias[None],
    )
    return encoded.reshape((length,) + video.shape[2:])


def solution(mesh):
    placed = (P("tm", None, None, "tile", None), P("tm"), P(), P(), P(), P(), P(), P())
    return jax.shard_map(
        shards, mesh=mesh, in_specs=placed, out_specs=P("tm", None, "tile", None), check_vma=False
    )
```

```python
import functools

import jax
import jax.numpy as jnp
from jax import lax
from jax.experimental import pallas as pl
from jax.experimental.pallas import tpu as pltpu
from jax.sharding import PartitionSpec as P

GROUPS = 32
OWN = 16
CAP = 2
C = 128
ROWS = 8
COLS = 16
POS = ROWS * COLS
LEAD = 4
CHUNK = 8
EPSILON = 1e-06
HALF = 24
PITCH = 24
UNROLL = 4
PAIR_ROWS = CAP * 2 * POS
INFO_ROWS = 16
MIB = 1024 * 1024

f32 = jnp.float32
bf16 = jnp.bfloat16


def vmem():
    return pl.BlockSpec(memory_space=pltpu.VMEM)


def smem():
    return pl.BlockSpec(memory_space=pltpu.SMEM)


def hbm():
    return pl.BlockSpec(memory_space=pl.ANY)


def params(mib=16):
    return pltpu.CompilerParams(vmem_limit_bytes=mib * MIB)


def hbm_only():
    return pl.BlockSpec(memory_space=pltpu.HBM)


LOADS = 4


def send_kernel(
    slot_hbm, video_ref, out_ref, slot_ref, count, target, held, info, info_out, sems_in, sems_out
):
    slots = slot_ref.shape[0]
    owners = out_ref.shape[0]
    block_rows = PAIR_ROWS // CAP

    def load(part):
        at = pl.ds(part * (slots // LOADS), slots // LOADS)
        return pltpu.make_async_copy(video_ref.at[at], held.at[at], sems_in.at[part])

    def store(slot, owner, rank):
        rows = pl.ds(pl.multiple_of(rank * block_rows, block_rows), block_rows)
        return pltpu.make_async_copy(
            held.at[slot], out_ref.at[owner, rows], sems_out.at[slot]
        )

    to_scalars = pltpu.make_async_copy(slot_hbm, slot_ref, sems_in.at[LOADS])
    to_scalars.start()
    for part in range(LOADS):
        load(part).start()
    for owner in range(owners + 1):
        count[owner] = 0
    info[...] = jnp.zeros_like(info)
    lane = lax.broadcasted_iota(jnp.int32, info.shape[1:], 1)
    to_scalars.wait()
    for slot in range(slots):
        block = slot_ref[slot]
        owner = jnp.where(block >= 0, block >> 4, owners)
        rank = count[owner]
        count[owner] = rank + 1
        target[slot] = rank
        mark = jnp.where(lane == (block & (OWN - 1)), (rank + 1).astype(f32), 0.0)
        info[owner] = info[owner] + mark
    for owner in range(owners):
        info_out[owner] = jnp.concatenate([info[owner]] * 2, axis=0).astype(bf16)
    notes = pltpu.make_async_copy(
        info_out, out_ref.at[:, pl.ds(PAIR_ROWS, INFO_ROWS)], sems_out.at[slots]
    )
    notes.start()
    for slot in range(slots):
        if slot % (slots // LOADS) == 0:
            load(slot // (slots // LOADS)).wait()

        @pl.when(slot_ref[slot] >= 0)
        def _():
            store(slot, slot_ref[slot] >> 4, target[slot]).start()

    for slot in range(slots):

        @pl.when(slot_ref[slot] >= 0)
        def _():
            store(slot, 0, 0).wait()

    notes.wait()


def send_blocks(slot_block, video, owners):
    slots = video.shape[0]
    return pl.pallas_call(
        send_kernel,
        out_shape=jax.ShapeDtypeStruct((owners, PAIR_ROWS + INFO_ROWS, C), video.dtype),
        in_specs=[hbm_only(), hbm_only()],
        out_specs=hbm_only(),
        scratch_shapes=[
            pltpu.SMEM((slots,), jnp.int32),
            pltpu.SMEM((owners + 1,), jnp.int32),
            pltpu.SMEM((slots,), jnp.int32),
            pltpu.VMEM((slots, PAIR_ROWS // CAP, C), bf16),
            pltpu.VMEM((owners + 1, 8, C), f32),
            pltpu.VMEM((owners, INFO_ROWS, C), bf16),
            pltpu.SemaphoreType.DMA((LOADS + 1,)),
            pltpu.SemaphoreType.DMA((slots + 1,)),
        ],
        compiler_params=params(62),
        name="send_blocks",
    )(slot_block, video.reshape(slots, PAIR_ROWS // CAP, C))


def order_kernel(arrived_ref, *refs):
    order_ref, tail_ref, picks, sem = refs[-4:]
    total = jnp.zeros((INFO_ROWS, C), f32)
    for source in range(arrived_ref.shape[0]):
        rank = arrived_ref[source, PAIR_ROWS:].astype(f32)
        total = total + jnp.where(rank > 0.0, rank + (CAP * source - 1.0), 0.0)
    picks[...] = total[0:8].astype(jnp.int32)
    to_scalars = pltpu.make_async_copy(picks.at[pl.ds(0, 1)], order_ref, sem)
    to_scalars.start()
    to_scalars.wait()
    for k in range(LEAD // 2):
        block = block_at(arrived_ref, order_ref[0, OWN - LEAD // 2 + k])
        tail_ref[k * 2 * POS : (k + 1) * 2 * POS] = block


def block_at(arrived_ref, arrival):
    block_rows = PAIR_ROWS // CAP
    rows = pl.ds(pl.multiple_of((arrival & 1) * block_rows, block_rows), block_rows)
    return arrived_ref[arrival >> 1, rows]


def block_order(arrived, ready):
    return pl.pallas_call(
        order_kernel,
        out_shape=(
            jax.ShapeDtypeStruct((1, C), jnp.int32),
            jax.ShapeDtypeStruct((LEAD * POS, C), bf16),
        ),
        in_specs=[vmem()] + [hbm()] * len(ready),
        out_specs=(smem(), vmem()),
        scratch_shapes=[pltpu.VMEM((8, C), jnp.int32), pltpu.SemaphoreType.DMA],
        compiler_params=params(),
        name="block_order",
    )(arrived, *ready)


def edge_rows(wide, column):
    return wide[pl.ds(column, wide.shape[0] // COLS, stride=COLS), :]


EDGE_ROWS = (LEAD + 2 * OWN) * ROWS


def put_edges(wide, start, left_ref, right_ref):
    count = wide.shape[0] // COLS
    for c in range(2):
        at = pl.ds(c * EDGE_ROWS + start, count)
        left_ref[at] = edge_rows(wide, c).astype(bf16)
        right_ref[at] = edge_rows(wide, COLS - 2 + c).astype(bf16)


def place_kernel(order_ref, arrived_ref, frames_ref, left_ref, right_ref, wide):
    for k in range(OWN):
        block = block_at(arrived_ref, order_ref[0, k])
        frames_ref[k * 2 * POS : (k + 1) * 2 * POS] = block
        wide[k % 2] = block.astype(f32)
        put_edges(wide.at[k % 2], (LEAD + 2 * k) * ROWS, left_ref, right_ref)


def edge_shape(dtype):
    return jax.ShapeDtypeStruct((2 * EDGE_ROWS, C), dtype)


def place_blocks(order, arrived):
    edge = edge_shape(bf16)
    return pl.pallas_call(
        place_kernel,
        out_shape=(jax.ShapeDtypeStruct((2 * OWN * POS, C), bf16), edge, edge),
        in_specs=[smem(), vmem()],
        out_specs=(vmem(), vmem(), vmem()),
        scratch_shapes=[pltpu.VMEM((2, 2 * POS, C), f32)],
        compiler_params=params(),
        name="place_blocks",
    )(order, arrived)


def lead_kernel(lead_ref, left_in, right_in, left_ref, right_ref, wide):
    wide[...] = lead_ref[...].astype(f32)
    left_ref[...] = left_in[...]
    right_ref[...] = right_in[...]
    put_edges(wide, 0, left_ref, right_ref)


def lead_edges(lead, left, right):
    edge = edge_shape(bf16)
    return pl.pallas_call(
        lead_kernel,
        out_shape=(edge, edge),
        in_specs=[vmem()] * 3,
        out_specs=(vmem(), vmem()),
        scratch_shapes=[pltpu.VMEM((LEAD * POS, C), f32)],
        compiler_params=params(),
        name="lead_edges",
    )(lead, left, right)


def join_kernel(first_ref, second_ref, edge_out, near1, far1, near2, far2, token_out):
    token_out[...] = jnp.zeros_like(token_out)
    for j in range(3):
        for i in range(3):
            at = (3 * j + i) * C
            for lag in range(3):
                lane = slice(lag * C, (lag + 1) * C)
                edge_out[at : at + C, lane] = first_ref[2 - lag, i, j]
                if lag < 2:
                    near1[at : at + C, lane] = first_ref[2 - lag, i, j]
                    near2[at : at + C, lane] = second_ref[2 - lag, i, j]
        for weight_ref, far in ((first_ref, far1), (second_ref, far2)):
            for i in range(4):
                for parity in range(2):
                    at = (4 * j + i) * C
                    inside = 0 <= i - parity <= 2
                    far[at : at + C, parity * C : (parity + 1) * C] = (
                        weight_ref[0, i - parity, j] if inside else jnp.zeros((C, C), bf16)
                    )


def join_weights(first, second):
    shapes = ((9 * C, 3 * C),) + ((9 * C, 2 * C), (12 * C, 2 * C)) * 2
    return pl.pallas_call(
        join_kernel,
        out_shape=tuple(jax.ShapeDtypeStruct(shape, bf16) for shape in shapes)
        + (jax.ShapeDtypeStruct((8, C), f32),),
        in_specs=[vmem()] * 2,
        out_specs=(vmem(),) * 6,
        compiler_params=params(),
        name="join_weights",
    )(first, second)


def conv_chunk(valid_ref, start, count, wide, taps, near, far, carry):
    for at in range(count * ROWS):
        q, r = at // ROWS, at % ROWS + 1
        base = at * PITCH + 8
        for j in range(3):
            taps[j, q, r] = wide[base + j - 1 : base + j - 1 + COLS].astype(bf16)
    windows = jnp.concatenate(
        [
            taps[j, 0:count, i : i + ROWS].reshape(count * POS, C)
            for j in range(3)
            for i in range(3)
        ],
        axis=1,
    )
    pairs = jnp.concatenate(
        [
            jnp.concatenate(
                [taps[j, q, i + 2 * p] for q in range(count) for p in range(ROWS // 2)], axis=0
            )
            for j in range(3)
            for i in range(4)
        ],
        axis=1,
    )
    product = jnp.dot(windows, near[...], preferred_element_type=f32)
    far_product = jnp.dot(pairs, far[...], preferred_element_type=f32)

    def part(q, lag):
        if lag < 2:
            return product[q * POS : (q + 1) * POS, lag * C : (lag + 1) * C]
        rows = []
        for r in range(ROWS):
            at = (q * (ROWS // 2) + r // 2) * COLS
            rows.append(far_product[at : at + COLS, (r % 2) * C : (r % 2 + 1) * C])
        return jnp.concatenate(rows, axis=0)

    totals = []
    for q in range(count):
        one = part(q - 1, 1) if q >= 1 else carry[0]
        two = part(q - 2, 2) if q >= 2 else carry[1 + q]
        totals.append(
            part(q, 0) + valid_ref[0, start + q] * one + valid_ref[1, start + q] * two
        )
    carry[0] = part(count - 1, 1)
    carry[1] = part(count - 2, 2)
    carry[2] = part(count - 1, 2)
    return totals


def conv_scratch():
    return [
        pltpu.VMEM((UNROLL, CHUNK * ROWS * PITCH + 8, C), f32),
        pltpu.VMEM((UNROLL, 3, CHUNK, ROWS + 2, COLS, C), bf16),
        pltpu.VMEM((3, POS, C), f32),
    ]


def conv_setup(taps, carry):
    carry[...] = jnp.zeros_like(carry)
    for u in range(UNROLL):
        for j in range(3):
            for edge in (0, ROWS + 1):
                taps[u, j, :, edge] = jnp.zeros((CHUNK, COLS, C), bf16)


def put_column(wide, at, column):
    wide[pl.ds(at, column.shape[0], stride=PITCH), :] = column


def over_chunks(chunk_step):
    def step(trip, done):
        for u in range(UNROLL):
            chunk_step(u, (trip * UNROLL + u) * CHUNK)
        return done

    lax.fori_loop(0, 2 * OWN // CHUNK // UNROLL, step, 0)


def group_total(entries):
    lane = lax.broadcasted_iota(jnp.int32, entries.shape, 1)
    for bit in (1, 2):
        up = pltpu.roll(entries, C - bit, 1)
        down = pltpu.roll(entries, bit, 1)
        entries = entries + jnp.where((lane & bit) == 0, up, down)
    return entries


def pick_columns(entries, picks):
    count = entries.shape[0]
    parts = []
    for _ in range(3):
        parts.append(entries.astype(bf16))
        entries = entries - parts[-1].astype(f32)
    picked = jnp.dot(
        jnp.concatenate(parts, axis=0), picks.astype(bf16), preferred_element_type=f32
    )
    return picked[0:count] + picked[count : 2 * count] + picked[2 * count :]


INNER = ROWS * (COLS - 2)


def hidden_kernel(
    valid_ref, lead_ref, frames_ref, near, far, hidden_ref, means_ref, spreads_ref,
    wide, taps, carry,
):
    conv_setup(taps, carry)
    none = jnp.zeros((CHUNK * ROWS, C), f32)
    for u in range(UNROLL):
        put_column(wide.at[u], 7, none)
        put_column(wide.at[u], 8 + COLS, none)
    means_ref[...] = jnp.zeros_like(means_ref)
    spreads_ref[...] = jnp.zeros_like(spreads_ref)
    column = lax.broadcasted_iota(jnp.int32, (POS, C), 0) % COLS
    inner = (column > 0) & (column < COLS - 1)

    def chunk_step(u, start, count, source, at):
        for row in range(count * ROWS):
            here = source[pl.ds(pl.multiple_of(at + row * COLS, COLS), COLS)]
            wide[u, row * PITCH + 8 : row * PITCH + 8 + COLS] = here.astype(f32)
        totals = conv_chunk(valid_ref, start, count, wide.at[u], taps.at[u], near, far, carry)
        for q in range(count):
            frame = start + q
            own = totals[q]
            hidden_ref[frame] = own
            mean = jnp.sum(jnp.where(inner, own, 0.0), axis=0, keepdims=True) / INNER
            centred = jnp.where(inner, own - mean, 0.0)
            means_ref[pl.ds(frame, 1), :] = mean
            spreads_ref[pl.ds(frame, 1), :] = jnp.sum(centred * centred, axis=0, keepdims=True)

    chunk_step(0, 0, LEAD, lead_ref, 0)
    over_chunks(lambda u, at: chunk_step(u, LEAD + at, CHUNK, frames_ref, at * POS))


def first_layer(valid, lead, frames, near, far):
    length = LEAD + 2 * OWN
    sums = jax.ShapeDtypeStruct((2 * HALF, C), f32)
    return pl.pallas_call(
        hidden_kernel,
        out_shape=(jax.ShapeDtypeStruct((length, POS, C), f32), sums, sums),
        in_specs=[smem()] + [vmem()] * 4,
        out_specs=(vmem(),) * 3,
        scratch_shapes=conv_scratch(),
        compiler_params=params(),
        cost_estimate=pl.CostEstimate(
            flops=2 * length * POS * 27 * C * C, bytes_accessed=4 * MIB, transcendentals=0
        ),
        name="first_layer",
    )(valid, lead, frames, near, far)


def edge_kernel(
    valid_ref, own_l, own_r, halo_l, halo_r, joined, means_ref, spreads_ref,
    edges_ref, stats_ref, means, spreads,
):
    row = lax.broadcasted_iota(jnp.int32, (EDGE_ROWS, C), 0) % ROWS
    length = EDGE_ROWS // ROWS

    def rows_of(ref, c):
        column = ref[c * EDGE_ROWS : (c + 1) * EDGE_ROWS].astype(f32)
        above = jnp.where(row == 0, 0.0, pltpu.roll(column, 1, 0))
        below = jnp.where(row == ROWS - 1, 0.0, pltpu.roll(column, EDGE_ROWS - 1, 0))
        return [piece.astype(bf16) for piece in (above, column, below)]

    for side, refs in enumerate(((halo_l, own_l), (own_r, halo_r))):
        columns = [rows_of(ref, c) for ref in refs for c in range(2)]
        for k in range(2):
            windows = jnp.concatenate(sum(columns[k : k + 3], []), axis=1)
            product = jnp.dot(windows, joined[...], preferred_element_type=f32)

            def part(frame, lag):
                rows = slice(frame * ROWS, (frame + 1) * ROWS)
                return product[rows, lag * C : (lag + 1) * C]

            at = 2 * side + k
            edges_ref[at, 0 : 2 * ROWS] = jnp.zeros((2 * ROWS, C), f32)
            for frame in range(2, length):
                edges_ref[at, frame * ROWS : (frame + 1) * ROWS] = (
                    part(frame, 0)
                    + valid_ref[0, frame] * part(frame - 1, 1)
                    + valid_ref[1, frame] * part(frame - 2, 2)
                )

    means[...] = jnp.zeros_like(means)
    spreads[...] = jnp.zeros_like(spreads)
    outer = [edges_ref[at].reshape(length, ROWS, C) for at in (1, 2)]
    mean = jnp.sum(outer[0] + outer[1], axis=1, keepdims=True) / (2 * ROWS)
    apart = [(entries - mean) * (entries - mean) for entries in outer]
    means[0:length] = mean.reshape(length, C)
    spreads[0:length] = jnp.sum(apart[0] + apart[1], axis=1)
    off = means[...] - means_ref[...]
    local = means_ref[...] + off * (2 * ROWS / POS)
    spread = spreads_ref[...] + spreads[...] + off * off * (INNER * 2 * ROWS / POS)

    mean = group_total(local) / 4
    off = local - mean
    spread = group_total(spread + POS * off * off)
    pieces = (mean[:HALF], spread[:HALF], mean[HALF:], spread[HALF:])
    channel = lax.broadcasted_iota(jnp.int32, (4 * C, C), 0)
    lane = lax.broadcasted_iota(jnp.int32, (4 * C, C), 1)
    picks = channel == C * (lane // GROUPS) + (C // GROUPS) * (lane % GROUPS)
    packed = pick_columns(jnp.concatenate(pieces, axis=1), picks.astype(f32))
    for peer in range(stats_ref.shape[0]):
        stats_ref[peer] = packed


def finish_hidden(valid, own_l, own_r, halo_l, halo_r, joined, means, spreads, tiles):
    return pl.pallas_call(
        edge_kernel,
        out_shape=(
            jax.ShapeDtypeStruct((4, EDGE_ROWS, C), f32),
            jax.ShapeDtypeStruct((tiles, HALF, C), f32),
        ),
        in_specs=[smem()] + [vmem()] * 7,
        out_specs=(vmem(),) * 2,
        scratch_shapes=[pltpu.VMEM((2 * HALF, C), f32), pltpu.VMEM((2 * HALF, C), f32)],
        compiler_params=params(),
        name="finish_hidden",
    )(valid, own_l, own_r, halo_l, halo_r, joined, means, spreads)


def combine_stats(stats_ref, gain_ref, means, scales):
    tiles = stats_ref.shape[0]
    here = POS * (C // GROUPS)
    lane = lax.broadcasted_iota(jnp.int32, (HALF, C), 1)
    is_mean = (lane // GROUPS) % 2 == 0
    total = stats_ref[0]
    for peer in range(1, tiles):
        total = total + stats_ref[peer]
    mean = total / tiles
    apart = jnp.zeros((HALF, C), f32)
    for peer in range(tiles):
        off = stats_ref[peer] - mean
        apart = apart + off * off
    apart = jnp.where(is_mean, apart, 0.0)
    variance = (total + here * pltpu.roll(apart, GROUPS, 1)) / (here * tiles)
    packed = jnp.where(is_mean, mean, lax.rsqrt(jnp.where(is_mean, 1.0, variance) + EPSILON))
    source = lax.broadcasted_iota(jnp.int32, (C, 4 * C), 0)
    column = lax.broadcasted_iota(jnp.int32, (C, 4 * C), 1)
    picks = source == GROUPS * (column // C) + (column % C) // (C // GROUPS)
    spread_out = pick_columns(packed, picks.astype(f32))
    means[0:HALF] = spread_out[:, 0:C]
    scales[0:HALF] = spread_out[:, C : 2 * C]
    means[HALF:] = spread_out[:, 2 * C : 3 * C]
    scales[HALF:] = spread_out[:, 3 * C :]
    scales[...] = scales[...] * gain_ref[...]


def silu(v):
    return v * (1.0 / (1.0 + jnp.exp(-v)))


def output_kernel(
    valid_ref, hidden_ref, edges_ref, stats_ref, frames_ref,
    gain_ref, norm_bias_ref, near, far, bias_ref, out_ref,
    wide, taps, carry, means, scales, halo, staged, sems,
):
    conv_setup(taps, carry)
    combine_stats(stats_ref, gain_ref, means, scales)
    has_left = valid_ref[2, 0]
    has_right = valid_ref[2, 1]

    def norm(hidden, frame):
        centred = hidden - means[pl.ds(frame, 1), :]
        return silu(centred * scales[pl.ds(frame, 1), :] + norm_bias_ref[...])

    def chunk_step(u, start, count):
        for q in range(count):
            frame = start + q
            active = norm(hidden_ref[frame], frame)
            for r in range(ROWS):
                at = (q * ROWS + r) * PITCH + 8
                wide[u, at : at + COLS] = active[r * COLS : (r + 1) * COLS]
            at = pl.ds(pl.multiple_of(frame * ROWS, ROWS), ROWS)
            for k, inside in enumerate((has_left, 1.0, 1.0, has_right)):
                halo[u, k, q * ROWS : (q + 1) * ROWS] = norm(edges_ref[k, at], frame) * inside
        for k, column in enumerate((7, 8, 7 + COLS, 8 + COLS)):
            put_column(wide.at[u], column, halo[u, k, 0 : count * ROWS])
        return conv_chunk(valid_ref, start, count, wide.at[u], taps.at[u], near, far, carry)

    def own_chunk(u, start):
        totals = chunk_step(u, LEAD + start, CHUNK)
        for q in range(CHUNK):
            rows = pl.ds(pl.multiple_of((start + q) * POS, POS), POS)
            total = frames_ref[rows].astype(f32) + (totals[q] + bias_ref[...])
            staged[rows] = total.astype(bf16)
        copy_out(start).start()

    def copy_out(start):
        rows = pl.ds(pl.multiple_of(start * POS, CHUNK * POS), CHUNK * POS)
        sem = sems.at[lax.div(jnp.int32(start), jnp.int32(CHUNK))]
        return pltpu.make_async_copy(staged.at[rows], out_ref.at[rows], sem)

    chunk_step(0, LEAD - 2, 2)
    over_chunks(own_chunk)
    for start in range(0, 2 * OWN, CHUNK):
        copy_out(start).wait()


def second_layer(valid, hidden, edges, stats, frames, gain, norm_bias, near, far, bias):
    return pl.pallas_call(
        output_kernel,
        out_shape=jax.ShapeDtypeStruct(frames.shape, bf16),
        in_specs=[smem()] + [vmem()] * 9,
        out_specs=hbm_only(),
        scratch_shapes=conv_scratch()
        + [
            pltpu.VMEM((2 * HALF, C), f32),
            pltpu.VMEM((2 * HALF, C), f32),
            pltpu.VMEM((UNROLL, 4, CHUNK * ROWS, C), f32),
            pltpu.VMEM(frames.shape, bf16),
            pltpu.SemaphoreType.DMA((2 * OWN // CHUNK,)),
        ],
        compiler_params=params(),
        name="second_layer",
    )(valid, hidden, edges, stats, frames, gain, norm_bias, near, far, bias)


def lag_masks(clip_frames, first_frame, length):
    clip_ends = jnp.cumsum(clip_frames)

    def clip_of(frames):
        ids = jnp.sum((frames[:, None] >= clip_ends[None, :]).astype(jnp.int32), axis=1)
        return jnp.where(frames < 0, -1, ids)

    frames = first_frame + jnp.arange(length, dtype=jnp.int32)
    here = clip_of(frames)
    return jnp.stack([clip_of(frames - lag) == here for lag in (1, 2)])


def swap_edges(left, right):
    count = lax.axis_size("tile")
    from_left = lax.ppermute(right, "tile", [(i, i + 1) for i in range(count - 1)])
    from_right = lax.ppermute(left, "tile", [(i + 1, i) for i in range(count - 1)])
    return from_left, from_right


def shards(
    video, slot_block, clip_frames, conv1_weight, norm_gain, norm_bias, conv2_weight, conv2_bias
):
    owners = lax.axis_size("tm")
    tiles = lax.axis_size("tile")
    position = lax.axis_index("tm")
    tile = lax.axis_index("tile")
    length = 2 * OWN

    outgoing = send_blocks(slot_block, video, owners)
    arrived = lax.all_to_all(outgoing, "tm", split_axis=0, concat_axis=0, tiled=True)

    inside = jnp.stack([tile > 0, tile < tiles - 1] + [tile < 0] * (length + LEAD - 2))
    valid = jnp.concatenate(
        [lag_masks(clip_frames, position * length - LEAD, length + LEAD), inside[None]]
    ).astype(f32)

    weight_edge, near1, far1, near2, far2, token = join_weights(conv1_weight, conv2_weight)
    order, tail = block_order(arrived, (valid, token))
    lead = lax.ppermute(tail, "tm", [(i, i + 1) for i in range(owners - 1)])
    frames, left, right = place_blocks(order, arrived)
    left, right = lead_edges(lead, left, right)
    from_left, from_right = swap_edges(left, right)
    hidden, means, spreads = first_layer(valid, lead, frames, near1, far1)
    edges, stats = finish_hidden(
        valid, left, right, from_left, from_right, weight_edge, means, spreads, tiles
    )
    stats = lax.all_to_all(stats, "tile", split_axis=0, concat_axis=0, tiled=True)
    encoded = second_layer(
        valid, hidden, edges, stats, frames, norm_gain[None], norm_bias[None],
        near2, far2, conv2_bias[None],
    )
    return encoded.reshape((length,) + video.shape[2:])


def solution(mesh):
    placed = (P("tm", None, None, "tile", None), P("tm"), P(), P(), P(), P(), P(), P())
    return jax.shard_map(
        shards, mesh=mesh, in_specs=placed, out_specs=P("tm", None, "tile", None), check_vma=False
    )
```

```python
import functools

import jax
import jax.numpy as jnp
from jax import lax
from jax.experimental import pallas as pl
from jax.experimental.pallas import tpu as pltpu
from jax.sharding import PartitionSpec as P

GROUPS = 32
OWN = 16
CAP = 2
C = 128
ROWS = 8
COLS = 16
POS = ROWS * COLS
LEAD = 4
CHUNK = 8
EPSILON = 1e-06
HALF = 24
PITCH = 24
UNROLL = 4
PAIR_ROWS = CAP * 2 * POS
INFO_ROWS = 16
MIB = 1024 * 1024

f32 = jnp.float32
bf16 = jnp.bfloat16


def vmem():
    return pl.BlockSpec(memory_space=pltpu.VMEM)


def smem():
    return pl.BlockSpec(memory_space=pltpu.SMEM)


def hbm():
    return pl.BlockSpec(memory_space=pl.ANY)


def params(mib=16):
    return pltpu.CompilerParams(vmem_limit_bytes=mib * MIB)


def hbm_only():
    return pl.BlockSpec(memory_space=pltpu.HBM)


LOADS = 4


def send_kernel(
    slot_hbm, video_ref, out_ref, slot_ref, count, target, held, info, info_out, sems_in, sems_out
):
    slots = slot_ref.shape[0]
    owners = out_ref.shape[0]
    block_rows = PAIR_ROWS // CAP

    def load(part):
        at = pl.ds(part * (slots // LOADS), slots // LOADS)
        return pltpu.make_async_copy(video_ref.at[at], held.at[at], sems_in.at[part])

    def store(slot, owner, rank):
        rows = pl.ds(pl.multiple_of(rank * block_rows, block_rows), block_rows)
        return pltpu.make_async_copy(
            held.at[slot], out_ref.at[owner, rows], sems_out.at[slot]
        )

    to_scalars = pltpu.make_async_copy(slot_hbm, slot_ref, sems_in.at[LOADS])
    to_scalars.start()
    for part in range(LOADS):
        load(part).start()
    for owner in range(owners + 1):
        count[owner] = 0
    info[...] = jnp.zeros_like(info)
    lane = lax.broadcasted_iota(jnp.int32, info.shape[1:], 1)
    to_scalars.wait()
    for slot in range(slots):
        block = slot_ref[slot]
        owner = jnp.where(block >= 0, block >> 4, owners)
        rank = count[owner]
        count[owner] = rank + 1
        target[slot] = rank
        mark = jnp.where(lane == (block & (OWN - 1)), (rank + 1).astype(f32), 0.0)
        info[owner] = info[owner] + mark
    for owner in range(owners):
        info_out[owner] = jnp.concatenate([info[owner]] * 2, axis=0).astype(bf16)
    notes = pltpu.make_async_copy(
        info_out, out_ref.at[:, pl.ds(PAIR_ROWS, INFO_ROWS)], sems_out.at[slots]
    )
    notes.start()
    for slot in range(slots):
        if slot % (slots // LOADS) == 0:
            load(slot // (slots // LOADS)).wait()

        @pl.when(slot_ref[slot] >= 0)
        def _():
            store(slot, slot_ref[slot] >> 4, target[slot]).start()

    for slot in range(slots):

        @pl.when(slot_ref[slot] >= 0)
        def _():
            store(slot, 0, 0).wait()

    notes.wait()


def send_blocks(slot_block, video, owners):
    slots = video.shape[0]
    return pl.pallas_call(
        send_kernel,
        out_shape=jax.ShapeDtypeStruct((owners, PAIR_ROWS + INFO_ROWS, C), video.dtype),
        in_specs=[hbm_only(), hbm_only()],
        out_specs=hbm_only(),
        scratch_shapes=[
            pltpu.SMEM((slots,), jnp.int32),
            pltpu.SMEM((owners + 1,), jnp.int32),
            pltpu.SMEM((slots,), jnp.int32),
            pltpu.VMEM((slots, PAIR_ROWS // CAP, C), bf16),
            pltpu.VMEM((owners + 1, 8, C), f32),
            pltpu.VMEM((owners, INFO_ROWS, C), bf16),
            pltpu.SemaphoreType.DMA((LOADS + 1,)),
            pltpu.SemaphoreType.DMA((slots + 1,)),
        ],
        compiler_params=params(62),
        name="send_blocks",
    )(slot_block, video.reshape(slots, PAIR_ROWS // CAP, C))


def order_kernel(arrived_ref, *refs):
    order_ref, tail_ref, picks, sem = refs[-4:]
    total = jnp.zeros((INFO_ROWS, C), f32)
    for source in range(arrived_ref.shape[0]):
        rank = arrived_ref[source, PAIR_ROWS:].astype(f32)
        total = total + jnp.where(rank > 0.0, rank + (CAP * source - 1.0), 0.0)
    picks[...] = total[0:8].astype(jnp.int32)
    to_scalars = pltpu.make_async_copy(picks.at[pl.ds(0, 1)], order_ref, sem)
    to_scalars.start()
    lane = lax.broadcasted_iota(jnp.int32, (8, C), 1)
    for k in range(LEAD // 2):
        arrival = jnp.max(jnp.where(lane == OWN - LEAD // 2 + k, total[0:8], 0.0))
        block = block_at(arrived_ref, arrival.astype(jnp.int32))
        tail_ref[k * 2 * POS : (k + 1) * 2 * POS] = block
    to_scalars.wait()


def block_at(arrived_ref, arrival):
    block_rows = PAIR_ROWS // CAP
    rows = pl.ds(pl.multiple_of((arrival & 1) * block_rows, block_rows), block_rows)
    return arrived_ref[arrival >> 1, rows]


def block_order(arrived, ready):
    return pl.pallas_call(
        order_kernel,
        out_shape=(
            jax.ShapeDtypeStruct((1, C), jnp.int32),
            jax.ShapeDtypeStruct((LEAD * POS, C), bf16),
        ),
        in_specs=[vmem()] + [hbm()] * len(ready),
        out_specs=(smem(), vmem()),
        scratch_shapes=[pltpu.VMEM((8, C), jnp.int32), pltpu.SemaphoreType.DMA],
        compiler_params=params(),
        name="block_order",
    )(arrived, *ready)


def edge_rows(wide, column):
    return wide[pl.ds(column, wide.shape[0] // COLS, stride=COLS), :]


EDGE_ROWS = (LEAD + 2 * OWN) * ROWS


def put_edges(wide, start, left_ref, right_ref):
    count = wide.shape[0] // COLS
    for c in range(2):
        at = pl.ds(c * EDGE_ROWS + start, count)
        left_ref[at] = edge_rows(wide, c).astype(bf16)
        right_ref[at] = edge_rows(wide, COLS - 2 + c).astype(bf16)


def own_kernel(order_ref, arrived_ref, left_ref, right_ref, wide):
    for k in range(OWN):
        wide[k % 2] = block_at(arrived_ref, order_ref[0, k]).astype(f32)
        put_edges(wide.at[k % 2], (LEAD + 2 * k) * ROWS, left_ref, right_ref)


def edge_shape(dtype):
    return jax.ShapeDtypeStruct((2 * EDGE_ROWS, C), dtype)


def own_edges(order, arrived):
    edge = edge_shape(bf16)
    return pl.pallas_call(
        own_kernel,
        out_shape=(edge, edge),
        in_specs=[smem(), vmem()],
        out_specs=(vmem(), vmem()),
        scratch_shapes=[pltpu.VMEM((2, 2 * POS, C), f32)],
        compiler_params=params(),
        name="own_edges",
    )(order, arrived)


def lead_kernel(lead_ref, left_in, right_in, left_ref, right_ref, wide):
    wide[...] = lead_ref[...].astype(f32)
    left_ref[...] = left_in[...]
    right_ref[...] = right_in[...]
    put_edges(wide, 0, left_ref, right_ref)


def lead_edges(lead, left, right):
    edge = edge_shape(bf16)
    return pl.pallas_call(
        lead_kernel,
        out_shape=(edge, edge),
        in_specs=[vmem()] * 3,
        out_specs=(vmem(), vmem()),
        scratch_shapes=[pltpu.VMEM((LEAD * POS, C), f32)],
        compiler_params=params(),
        name="lead_edges",
    )(lead, left, right)


def join_kernel(first_ref, second_ref, edge_out, near1, far1, near2, far2, token_out):
    token_out[...] = jnp.zeros_like(token_out)
    for j in range(3):
        for i in range(3):
            at = (3 * j + i) * C
            for lag in range(3):
                lane = slice(lag * C, (lag + 1) * C)
                edge_out[at : at + C, lane] = first_ref[2 - lag, i, j]
                if lag < 2:
                    near1[at : at + C, lane] = first_ref[2 - lag, i, j]
                    near2[at : at + C, lane] = second_ref[2 - lag, i, j]
        for weight_ref, far in ((first_ref, far1), (second_ref, far2)):
            for i in range(4):
                for parity in range(2):
                    at = (4 * j + i) * C
                    inside = 0 <= i - parity <= 2
                    far[at : at + C, parity * C : (parity + 1) * C] = (
                        weight_ref[0, i - parity, j] if inside else jnp.zeros((C, C), bf16)
                    )


def join_weights(first, second):
    shapes = ((9 * C, 3 * C),) + ((9 * C, 2 * C), (12 * C, 2 * C)) * 2
    return pl.pallas_call(
        join_kernel,
        out_shape=tuple(jax.ShapeDtypeStruct(shape, bf16) for shape in shapes)
        + (jax.ShapeDtypeStruct((8, C), f32),),
        in_specs=[vmem()] * 2,
        out_specs=(vmem(),) * 6,
        compiler_params=params(),
        name="join_weights",
    )(first, second)


def conv_chunk(valid_ref, start, count, wide, taps, near, far, carry):
    for at in range(count * ROWS):
        q, r = at // ROWS, at % ROWS + 1
        base = at * PITCH + 8
        for j in range(3):
            taps[j, q, r] = wide[base + j - 1 : base + j - 1 + COLS].astype(bf16)
    windows = jnp.concatenate(
        [
            taps[j, 0:count, i : i + ROWS].reshape(count * POS, C)
            for j in range(3)
            for i in range(3)
        ],
        axis=1,
    )
    pairs = jnp.concatenate(
        [
            jnp.concatenate(
                [taps[j, q, i + 2 * p] for q in range(count) for p in range(ROWS // 2)], axis=0
            )
            for j in range(3)
            for i in range(4)
        ],
        axis=1,
    )
    product = jnp.dot(windows, near[...], preferred_element_type=f32)
    far_product = jnp.dot(pairs, far[...], preferred_element_type=f32)

    def part(q, lag):
        if lag < 2:
            return product[q * POS : (q + 1) * POS, lag * C : (lag + 1) * C]
        rows = []
        for r in range(ROWS):
            at = (q * (ROWS // 2) + r // 2) * COLS
            rows.append(far_product[at : at + COLS, (r % 2) * C : (r % 2 + 1) * C])
        return jnp.concatenate(rows, axis=0)

    totals = []
    for q in range(count):
        one = part(q - 1, 1) if q >= 1 else carry[0]
        two = part(q - 2, 2) if q >= 2 else carry[1 + q]
        totals.append(
            part(q, 0) + valid_ref[0, start + q] * one + valid_ref[1, start + q] * two
        )
    carry[0] = part(count - 1, 1)
    carry[1] = part(count - 2, 2)
    carry[2] = part(count - 1, 2)
    return totals


def conv_scratch():
    return [
        pltpu.VMEM((UNROLL, CHUNK * ROWS * PITCH + 8, C), f32),
        pltpu.VMEM((UNROLL, 3, CHUNK, ROWS + 2, COLS, C), bf16),
        pltpu.VMEM((3, POS, C), f32),
    ]


def conv_setup(taps, carry):
    carry[...] = jnp.zeros_like(carry)
    for u in range(UNROLL):
        for j in range(3):
            for edge in (0, ROWS + 1):
                taps[u, j, :, edge] = jnp.zeros((CHUNK, COLS, C), bf16)


def put_column(wide, at, column):
    wide[pl.ds(at, column.shape[0], stride=PITCH), :] = column


def over_chunks(chunk_step):
    def step(trip, done):
        for u in range(UNROLL):
            chunk_step(u, (trip * UNROLL + u) * CHUNK)
        return done

    lax.fori_loop(0, 2 * OWN // CHUNK // UNROLL, step, 0)


def group_total(entries):
    lane = lax.broadcasted_iota(jnp.int32, entries.shape, 1)
    for bit in (1, 2):
        up = pltpu.roll(entries, C - bit, 1)
        down = pltpu.roll(entries, bit, 1)
        entries = entries + jnp.where((lane & bit) == 0, up, down)
    return entries


def pick_columns(entries, picks):
    count = entries.shape[0]
    parts = []
    for _ in range(3):
        parts.append(entries.astype(bf16))
        entries = entries - parts[-1].astype(f32)
    picked = jnp.dot(
        jnp.concatenate(parts, axis=0), picks.astype(bf16), preferred_element_type=f32
    )
    return picked[0:count] + picked[count : 2 * count] + picked[2 * count :]


INNER = ROWS * (COLS - 2)


def hidden_kernel(
    valid_ref, order_ref, lead_ref, arrived_ref, near, far, hidden_ref, means_ref, spreads_ref,
    wide, taps, carry,
):
    conv_setup(taps, carry)
    none = jnp.zeros((CHUNK * ROWS, C), f32)
    for u in range(UNROLL):
        put_column(wide.at[u], 7, none)
        put_column(wide.at[u], 8 + COLS, none)
    means_ref[...] = jnp.zeros_like(means_ref)
    spreads_ref[...] = jnp.zeros_like(spreads_ref)
    column = lax.broadcasted_iota(jnp.int32, (POS, C), 0) % COLS
    inner = (column > 0) & (column < COLS - 1)

    def chunk_step(u, start, count, block_of):
        for k in range(count // 2):
            block = block_of(k).astype(f32)
            for row in range(2 * ROWS):
                at = (k * 2 * ROWS + row) * PITCH + 8
                wide[u, at : at + COLS] = block[row * COLS : (row + 1) * COLS]
        totals = conv_chunk(valid_ref, start, count, wide.at[u], taps.at[u], near, far, carry)
        for q in range(count):
            frame = start + q
            own = totals[q]
            hidden_ref[frame] = own
            mean = jnp.sum(jnp.where(inner, own, 0.0), axis=0, keepdims=True) / INNER
            centred = jnp.where(inner, own - mean, 0.0)
            means_ref[pl.ds(frame, 1), :] = mean
            spreads_ref[pl.ds(frame, 1), :] = jnp.sum(centred * centred, axis=0, keepdims=True)

    def own_block(at):
        return lambda k: block_at(arrived_ref, order_ref[0, at // 2 + k])

    chunk_step(0, 0, LEAD, lambda k: lead_ref[k * 2 * POS : (k + 1) * 2 * POS])
    over_chunks(lambda u, at: chunk_step(u, LEAD + at, CHUNK, own_block(at)))


def first_layer(valid, order, lead, arrived, near, far):
    length = LEAD + 2 * OWN
    sums = jax.ShapeDtypeStruct((2 * HALF, C), f32)
    return pl.pallas_call(
        hidden_kernel,
        out_shape=(jax.ShapeDtypeStruct((length, POS, C), f32), sums, sums),
        in_specs=[smem()] * 2 + [vmem()] * 4,
        out_specs=(vmem(),) * 3,
        scratch_shapes=conv_scratch(),
        compiler_params=params(24),
        cost_estimate=pl.CostEstimate(
            flops=2 * length * POS * 27 * C * C, bytes_accessed=4 * MIB, transcendentals=0
        ),
        name="first_layer",
    )(valid, order, lead, arrived, near, far)


def edge_kernel(
    valid_ref, own_l, own_r, halo_l, halo_r, joined, means_ref, spreads_ref,
    edges_ref, stats_ref, means, spreads,
):
    row = lax.broadcasted_iota(jnp.int32, (EDGE_ROWS, C), 0) % ROWS
    length = EDGE_ROWS // ROWS

    def rows_of(ref, c):
        column = ref[c * EDGE_ROWS : (c + 1) * EDGE_ROWS].astype(f32)
        above = jnp.where(row == 0, 0.0, pltpu.roll(column, 1, 0))
        below = jnp.where(row == ROWS - 1, 0.0, pltpu.roll(column, EDGE_ROWS - 1, 0))
        return [piece.astype(bf16) for piece in (above, column, below)]

    for side, refs in enumerate(((halo_l, own_l), (own_r, halo_r))):
        columns = [rows_of(ref, c) for ref in refs for c in range(2)]
        for k in range(2):
            windows = jnp.concatenate(sum(columns[k : k + 3], []), axis=1)
            product = jnp.dot(windows, joined[...], preferred_element_type=f32)

            def part(frame, lag):
                rows = slice(frame * ROWS, (frame + 1) * ROWS)
                return product[rows, lag * C : (lag + 1) * C]

            at = 2 * side + k
            edges_ref[at, 0 : 2 * ROWS] = jnp.zeros((2 * ROWS, C), f32)
            for frame in range(2, length):
                edges_ref[at, frame * ROWS : (frame + 1) * ROWS] = (
                    part(frame, 0)
                    + valid_ref[0, frame] * part(frame - 1, 1)
                    + valid_ref[1, frame] * part(frame - 2, 2)
                )

    means[...] = jnp.zeros_like(means)
    spreads[...] = jnp.zeros_like(spreads)
    outer = [edges_ref[at].reshape(length, ROWS, C) for at in (1, 2)]
    mean = jnp.sum(outer[0] + outer[1], axis=1, keepdims=True) / (2 * ROWS)
    apart = [(entries - mean) * (entries - mean) for entries in outer]
    means[0:length] = mean.reshape(length, C)
    spreads[0:length] = jnp.sum(apart[0] + apart[1], axis=1)
    off = means[...] - means_ref[...]
    local = means_ref[...] + off * (2 * ROWS / POS)
    spread = spreads_ref[...] + spreads[...] + off * off * (INNER * 2 * ROWS / POS)

    mean = group_total(local) / 4
    off = local - mean
    spread = group_total(spread + POS * off * off)
    pieces = (mean[:HALF], spread[:HALF], mean[HALF:], spread[HALF:])
    channel = lax.broadcasted_iota(jnp.int32, (4 * C, C), 0)
    lane = lax.broadcasted_iota(jnp.int32, (4 * C, C), 1)
    picks = channel == C * (lane // GROUPS) + (C // GROUPS) * (lane % GROUPS)
    packed = pick_columns(jnp.concatenate(pieces, axis=1), picks.astype(f32))
    for peer in range(stats_ref.shape[0]):
        stats_ref[peer] = packed


def finish_hidden(valid, own_l, own_r, halo_l, halo_r, joined, means, spreads, tiles):
    return pl.pallas_call(
        edge_kernel,
        out_shape=(
            jax.ShapeDtypeStruct((4, EDGE_ROWS, C), f32),
            jax.ShapeDtypeStruct((tiles, HALF, C), f32),
        ),
        in_specs=[smem()] + [vmem()] * 7,
        out_specs=(vmem(),) * 2,
        scratch_shapes=[pltpu.VMEM((2 * HALF, C), f32), pltpu.VMEM((2 * HALF, C), f32)],
        compiler_params=params(),
        name="finish_hidden",
    )(valid, own_l, own_r, halo_l, halo_r, joined, means, spreads)


def combine_stats(stats_ref, gain_ref, means, scales):
    tiles = stats_ref.shape[0]
    here = POS * (C // GROUPS)
    lane = lax.broadcasted_iota(jnp.int32, (HALF, C), 1)
    is_mean = (lane // GROUPS) % 2 == 0
    total = stats_ref[0]
    for peer in range(1, tiles):
        total = total + stats_ref[peer]
    mean = total / tiles
    apart = jnp.zeros((HALF, C), f32)
    for peer in range(tiles):
        off = stats_ref[peer] - mean
        apart = apart + off * off
    apart = jnp.where(is_mean, apart, 0.0)
    variance = (total + here * pltpu.roll(apart, GROUPS, 1)) / (here * tiles)
    packed = jnp.where(is_mean, mean, lax.rsqrt(jnp.where(is_mean, 1.0, variance) + EPSILON))
    source = lax.broadcasted_iota(jnp.int32, (C, 4 * C), 0)
    column = lax.broadcasted_iota(jnp.int32, (C, 4 * C), 1)
    picks = source == GROUPS * (column // C) + (column % C) // (C // GROUPS)
    spread_out = pick_columns(packed, picks.astype(f32))
    means[0:HALF] = spread_out[:, 0:C]
    scales[0:HALF] = spread_out[:, C : 2 * C]
    means[HALF:] = spread_out[:, 2 * C : 3 * C]
    scales[HALF:] = spread_out[:, 3 * C :]
    scales[...] = scales[...] * gain_ref[...]


def silu(v):
    return v * (1.0 / (1.0 + jnp.exp(-v)))


def output_kernel(
    valid_ref, order_ref, hidden_ref, edges_ref, stats_ref, arrived_ref,
    gain_ref, norm_bias_ref, near, far, bias_ref, out_ref,
    wide, taps, carry, means, scales, halo, staged, sems,
):
    conv_setup(taps, carry)
    combine_stats(stats_ref, gain_ref, means, scales)
    has_left = valid_ref[2, 0]
    has_right = valid_ref[2, 1]

    def norm(hidden, frame):
        centred = hidden - means[pl.ds(frame, 1), :]
        return silu(centred * scales[pl.ds(frame, 1), :] + norm_bias_ref[...])

    def chunk_step(u, start, count):
        for q in range(count):
            frame = start + q
            active = norm(hidden_ref[frame], frame)
            for r in range(ROWS):
                at = (q * ROWS + r) * PITCH + 8
                wide[u, at : at + COLS] = active[r * COLS : (r + 1) * COLS]
            at = pl.ds(pl.multiple_of(frame * ROWS, ROWS), ROWS)
            for k, inside in enumerate((has_left, 1.0, 1.0, has_right)):
                halo[u, k, q * ROWS : (q + 1) * ROWS] = norm(edges_ref[k, at], frame) * inside
        for k, column in enumerate((7, 8, 7 + COLS, 8 + COLS)):
            put_column(wide.at[u], column, halo[u, k, 0 : count * ROWS])
        return conv_chunk(valid_ref, start, count, wide.at[u], taps.at[u], near, far, carry)

    def own_chunk(u, start):
        totals = chunk_step(u, LEAD + start, CHUNK)
        for k in range(CHUNK // 2):
            block = block_at(arrived_ref, order_ref[0, start // 2 + k]).astype(f32)
            total = block + (jnp.concatenate(totals[2 * k : 2 * k + 2], axis=0) + bias_ref[...])
            rows = pl.ds(pl.multiple_of((start + 2 * k) * POS, 2 * POS), 2 * POS)
            staged[rows] = total.astype(bf16)
        copy_out(start).start()

    def copy_out(start):
        rows = pl.ds(pl.multiple_of(start * POS, CHUNK * POS), CHUNK * POS)
        sem = sems.at[lax.div(jnp.int32(start), jnp.int32(CHUNK))]
        return pltpu.make_async_copy(staged.at[rows], out_ref.at[rows], sem)

    chunk_step(0, LEAD - 2, 2)
    over_chunks(own_chunk)
    for start in range(0, 2 * OWN, CHUNK):
        copy_out(start).wait()


def second_layer(valid, order, hidden, edges, stats, arrived, gain, norm_bias, near, far, bias):
    return pl.pallas_call(
        output_kernel,
        out_shape=jax.ShapeDtypeStruct((2 * OWN * POS, C), bf16),
        in_specs=[smem()] * 2 + [vmem()] * 9,
        out_specs=hbm_only(),
        scratch_shapes=conv_scratch()
        + [
            pltpu.VMEM((2 * HALF, C), f32),
            pltpu.VMEM((2 * HALF, C), f32),
            pltpu.VMEM((UNROLL, 4, CHUNK * ROWS, C), f32),
            pltpu.VMEM((2 * OWN * POS, C), bf16),
            pltpu.SemaphoreType.DMA((2 * OWN // CHUNK,)),
        ],
        compiler_params=params(24),
        name="second_layer",
    )(valid, order, hidden, edges, stats, arrived, gain, norm_bias, near, far, bias)


def lag_masks(clip_frames, first_frame, length):
    clip_ends = jnp.cumsum(clip_frames)

    def clip_of(frames):
        ids = jnp.sum((frames[:, None] >= clip_ends[None, :]).astype(jnp.int32), axis=1)
        return jnp.where(frames < 0, -1, ids)

    frames = first_frame + jnp.arange(length, dtype=jnp.int32)
    here = clip_of(frames)
    return jnp.stack([clip_of(frames - lag) == here for lag in (1, 2)])


def swap_edges(left, right):
    count = lax.axis_size("tile")
    from_left = lax.ppermute(right, "tile", [(i, i + 1) for i in range(count - 1)])
    from_right = lax.ppermute(left, "tile", [(i + 1, i) for i in range(count - 1)])
    return from_left, from_right


def shards(
    video, slot_block, clip_frames, conv1_weight, norm_gain, norm_bias, conv2_weight, conv2_bias
):
    owners = lax.axis_size("tm")
    tiles = lax.axis_size("tile")
    position = lax.axis_index("tm")
    tile = lax.axis_index("tile")
    length = 2 * OWN

    outgoing = send_blocks(slot_block, video, owners)
    arrived = lax.all_to_all(outgoing, "tm", split_axis=0, concat_axis=0, tiled=True)

    inside = jnp.stack([tile > 0, tile < tiles - 1] + [tile < 0] * (length + LEAD - 2))
    valid = jnp.concatenate(
        [lag_masks(clip_frames, position * length - LEAD, length + LEAD), inside[None]]
    ).astype(f32)

    weight_edge, near1, far1, near2, far2, token = join_weights(conv1_weight, conv2_weight)
    order, tail = block_order(arrived, (valid, token))
    lead = lax.ppermute(tail, "tm", [(i, i + 1) for i in range(owners - 1)])
    left, right = own_edges(order, arrived)
    left, right = lead_edges(lead, left, right)
    from_left, from_right = swap_edges(left, right)
    hidden, means, spreads = first_layer(valid, order, lead, arrived, near1, far1)
    edges, stats = finish_hidden(
        valid, left, right, from_left, from_right, weight_edge, means, spreads, tiles
    )
    stats = lax.all_to_all(stats, "tile", split_axis=0, concat_axis=0, tiled=True)
    encoded = second_layer(
        valid, order, hidden, edges, stats, arrived, norm_gain[None], norm_bias[None],
        near2, far2, conv2_bias[None],
    )
    return encoded.reshape((length,) + video.shape[2:])


def solution(mesh):
    placed = (P("tm", None, None, "tile", None), P("tm"), P(), P(), P(), P(), P(), P())
    return jax.shard_map(
        shards, mesh=mesh, in_specs=placed, out_specs=P("tm", None, "tile", None), check_vma=False
    )
```

```python
import functools

import jax
import jax.numpy as jnp
from jax import lax
from jax.experimental import pallas as pl
from jax.experimental.pallas import tpu as pltpu
from jax.sharding import PartitionSpec as P

GROUPS = 32
OWN = 16
CAP = 2
C = 128
ROWS = 8
COLS = 16
POS = ROWS * COLS
LEAD = 4
CHUNK = 8
EPSILON = 1e-06
HALF = 24
PITCH = 24
UNROLL = 4
PAIR_ROWS = CAP * 2 * POS
INFO_ROWS = 16
MIB = 1024 * 1024

f32 = jnp.float32
bf16 = jnp.bfloat16


def vmem():
    return pl.BlockSpec(memory_space=pltpu.VMEM)


def smem():
    return pl.BlockSpec(memory_space=pltpu.SMEM)


def hbm():
    return pl.BlockSpec(memory_space=pl.ANY)


def params(mib=16):
    return pltpu.CompilerParams(vmem_limit_bytes=mib * MIB)


def hbm_only():
    return pl.BlockSpec(memory_space=pltpu.HBM)


LOADS = 4


def send_kernel(
    slot_hbm, video_ref, out_ref, slot_ref, count, target, held, info, info_out, sems_in, sems_out
):
    slots = slot_ref.shape[0]
    owners = out_ref.shape[0]
    block_rows = PAIR_ROWS // CAP

    def load(part):
        at = pl.ds(part * (slots // LOADS), slots // LOADS)
        return pltpu.make_async_copy(video_ref.at[at], held.at[at], sems_in.at[part])

    def store(slot, owner, rank):
        rows = pl.ds(pl.multiple_of(rank * block_rows, block_rows), block_rows)
        return pltpu.make_async_copy(
            held.at[slot], out_ref.at[owner, rows], sems_out.at[slot]
        )

    to_scalars = pltpu.make_async_copy(slot_hbm, slot_ref, sems_in.at[LOADS])
    to_scalars.start()
    for part in range(LOADS):
        load(part).start()
    for owner in range(owners + 1):
        count[owner] = 0
    info[...] = jnp.zeros_like(info)
    lane = lax.broadcasted_iota(jnp.int32, info.shape[1:], 1)
    to_scalars.wait()
    for slot in range(slots):
        block = slot_ref[slot]
        owner = jnp.where(block >= 0, block >> 4, owners)
        rank = count[owner]
        count[owner] = rank + 1
        target[slot] = rank
        mark = jnp.where(lane == (block & (OWN - 1)), (rank + 1).astype(f32), 0.0)
        info[owner] = info[owner] + mark
    for owner in range(owners):
        info_out[owner] = jnp.concatenate([info[owner]] * 2, axis=0).astype(bf16)
    notes = pltpu.make_async_copy(
        info_out, out_ref.at[:, pl.ds(PAIR_ROWS, INFO_ROWS)], sems_out.at[slots]
    )
    notes.start()
    for slot in range(slots):
        if slot % (slots // LOADS) == 0:
            load(slot // (slots // LOADS)).wait()

        @pl.when(slot_ref[slot] >= 0)
        def _():
            store(slot, slot_ref[slot] >> 4, target[slot]).start()

    for slot in range(slots):

        @pl.when(slot_ref[slot] >= 0)
        def _():
            store(slot, 0, 0).wait()

    notes.wait()


def send_blocks(slot_block, video, owners):
    slots = video.shape[0]
    return pl.pallas_call(
        send_kernel,
        out_shape=jax.ShapeDtypeStruct((owners, PAIR_ROWS + INFO_ROWS, C), video.dtype),
        in_specs=[hbm_only(), hbm_only()],
        out_specs=hbm_only(),
        scratch_shapes=[
            pltpu.SMEM((slots,), jnp.int32),
            pltpu.SMEM((owners + 1,), jnp.int32),
            pltpu.SMEM((slots,), jnp.int32),
            pltpu.VMEM((slots, PAIR_ROWS // CAP, C), bf16),
            pltpu.VMEM((owners + 1, 8, C), f32),
            pltpu.VMEM((owners, INFO_ROWS, C), bf16),
            pltpu.SemaphoreType.DMA((LOADS + 1,)),
            pltpu.SemaphoreType.DMA((slots + 1,)),
        ],
        compiler_params=params(62),
        name="send_blocks",
    )(slot_block, video.reshape(slots, PAIR_ROWS // CAP, C))


def order_kernel(arrived_ref, *refs):
    order_ref, tail_ref, picks, sem = refs[-4:]
    total = jnp.zeros((INFO_ROWS, C), f32)
    for source in range(arrived_ref.shape[0]):
        rank = arrived_ref[source, PAIR_ROWS:].astype(f32)
        total = total + jnp.where(rank > 0.0, rank + (CAP * source - 1.0), 0.0)
    picks[...] = total[0:8].astype(jnp.int32)
    to_scalars = pltpu.make_async_copy(picks.at[pl.ds(0, 1)], order_ref, sem)
    to_scalars.start()
    lane = lax.broadcasted_iota(jnp.int32, (8, C), 1)
    for k in range(LEAD // 2):
        arrival = jnp.max(jnp.where(lane == OWN - LEAD // 2 + k, total[0:8], 0.0))
        block = block_at(arrived_ref, arrival.astype(jnp.int32))
        tail_ref[k * 2 * POS : (k + 1) * 2 * POS] = block
    to_scalars.wait()


def block_at(arrived_ref, arrival):
    block_rows = PAIR_ROWS // CAP
    rows = pl.ds(pl.multiple_of((arrival & 1) * block_rows, block_rows), block_rows)
    return arrived_ref[arrival >> 1, rows]


def block_order(arrived, ready):
    return pl.pallas_call(
        order_kernel,
        out_shape=(
            jax.ShapeDtypeStruct((1, C), jnp.int32),
            jax.ShapeDtypeStruct((LEAD * POS, C), bf16),
        ),
        in_specs=[vmem()] + [hbm()] * len(ready),
        out_specs=(smem(), vmem()),
        scratch_shapes=[pltpu.VMEM((8, C), jnp.int32), pltpu.SemaphoreType.DMA],
        compiler_params=params(),
        name="block_order",
    )(arrived, *ready)


def edge_rows(wide, column):
    return wide[pl.ds(column, wide.shape[0] // COLS, stride=COLS), :]


EDGE_ROWS = (LEAD + 2 * OWN) * ROWS


def put_edges(wide, start, left_ref, right_ref):
    count = wide.shape[0] // COLS
    for c in range(2):
        at = pl.ds(c * EDGE_ROWS + start, count)
        left_ref[at] = edge_rows(wide, c).astype(bf16)
        right_ref[at] = edge_rows(wide, COLS - 2 + c).astype(bf16)


def own_kernel(order_ref, arrived_ref, left_ref, right_ref, wide):
    for k in range(OWN):
        wide[k % 2] = block_at(arrived_ref, order_ref[0, k]).astype(f32)
        put_edges(wide.at[k % 2], (LEAD + 2 * k) * ROWS, left_ref, right_ref)


def edge_shape(dtype):
    return jax.ShapeDtypeStruct((2 * EDGE_ROWS, C), dtype)


def own_edges(order, arrived):
    edge = edge_shape(bf16)
    return pl.pallas_call(
        own_kernel,
        out_shape=(edge, edge),
        in_specs=[smem(), vmem()],
        out_specs=(vmem(), vmem()),
        scratch_shapes=[pltpu.VMEM((2, 2 * POS, C), f32)],
        compiler_params=params(),
        name="own_edges",
    )(order, arrived)


def lead_kernel(lead_ref, left_in, right_in, left_ref, right_ref, wide):
    wide[...] = lead_ref[...].astype(f32)
    left_ref[...] = left_in[...]
    right_ref[...] = right_in[...]
    put_edges(wide, 0, left_ref, right_ref)


def lead_edges(lead, left, right):
    edge = edge_shape(bf16)
    return pl.pallas_call(
        lead_kernel,
        out_shape=(edge, edge),
        in_specs=[vmem()] * 3,
        out_specs=(vmem(), vmem()),
        scratch_shapes=[pltpu.VMEM((LEAD * POS, C), f32)],
        compiler_params=params(),
        name="lead_edges",
    )(lead, left, right)


def join_kernel(first_ref, second_ref, edge_out, near1, far1, near2, far2, token_out):
    token_out[...] = jnp.zeros_like(token_out)
    for j in range(3):
        for i in range(3):
            at = (3 * j + i) * C
            for lag in range(3):
                lane = slice(lag * C, (lag + 1) * C)
                edge_out[at : at + C, lane] = first_ref[2 - lag, i, j]
                if lag < 2:
                    near1[at : at + C, lane] = first_ref[2 - lag, i, j]
                    near2[at : at + C, lane] = second_ref[2 - lag, i, j]
        for weight_ref, far in ((first_ref, far1), (second_ref, far2)):
            for i in range(4):
                for parity in range(2):
                    at = (4 * j + i) * C
                    inside = 0 <= i - parity <= 2
                    far[at : at + C, parity * C : (parity + 1) * C] = (
                        weight_ref[0, i - parity, j] if inside else jnp.zeros((C, C), bf16)
                    )


def join_weights(first, second):
    shapes = ((9 * C, 3 * C),) + ((9 * C, 2 * C), (12 * C, 2 * C)) * 2
    return pl.pallas_call(
        join_kernel,
        out_shape=tuple(jax.ShapeDtypeStruct(shape, bf16) for shape in shapes)
        + (jax.ShapeDtypeStruct((8, C), f32),),
        in_specs=[vmem()] * 2,
        out_specs=(vmem(),) * 6,
        compiler_params=params(),
        name="join_weights",
    )(first, second)


def conv_chunk(valid_ref, start, count, wide, taps, near, far, carry):
    for at in range(count * ROWS):
        q, r = at // ROWS, at % ROWS + 1
        base = at * PITCH + 8
        for j in range(3):
            taps[j, q, r] = wide[base + j - 1 : base + j - 1 + COLS].astype(bf16)
    windows = jnp.concatenate(
        [
            taps[j, 0:count, i : i + ROWS].reshape(count * POS, C)
            for j in range(3)
            for i in range(3)
        ],
        axis=1,
    )
    pairs = jnp.concatenate(
        [
            jnp.concatenate(
                [taps[j, q, i + 2 * p] for q in range(count) for p in range(ROWS // 2)], axis=0
            )
            for j in range(3)
            for i in range(4)
        ],
        axis=1,
    )
    product = jnp.dot(windows, near[...], preferred_element_type=f32)
    far_product = jnp.dot(pairs, far[...], preferred_element_type=f32)

    def part(q, lag):
        if lag < 2:
            return product[q * POS : (q + 1) * POS, lag * C : (lag + 1) * C]
        rows = []
        for r in range(ROWS):
            at = (q * (ROWS // 2) + r // 2) * COLS
            rows.append(far_product[at : at + COLS, (r % 2) * C : (r % 2 + 1) * C])
        return jnp.concatenate(rows, axis=0)

    totals = []
    for q in range(count):
        one = part(q - 1, 1) if q >= 1 else carry[0]
        two = part(q - 2, 2) if q >= 2 else carry[1 + q]
        totals.append(
            part(q, 0) + valid_ref[0, start + q] * one + valid_ref[1, start + q] * two
        )
    carry[0] = part(count - 1, 1)
    carry[1] = part(count - 2, 2)
    carry[2] = part(count - 1, 2)
    return totals


def conv_scratch():
    return [
        pltpu.VMEM((UNROLL, CHUNK * ROWS * PITCH + 8, C), f32),
        pltpu.VMEM((UNROLL, 3, CHUNK, ROWS + 2, COLS, C), bf16),
        pltpu.VMEM((3, POS, C), f32),
    ]


def conv_setup(taps, carry):
    carry[...] = jnp.zeros_like(carry)
    for u in range(UNROLL):
        for j in range(3):
            for edge in (0, ROWS + 1):
                taps[u, j, :, edge] = jnp.zeros((CHUNK, COLS, C), bf16)


def put_column(wide, at, column):
    wide[pl.ds(at, column.shape[0], stride=PITCH), :] = column


def over_chunks(chunk_step):
    def step(trip, done):
        for u in range(UNROLL):
            chunk_step(u, (trip * UNROLL + u) * CHUNK)
        return done

    trips = 2 * OWN // CHUNK // UNROLL
    if trips == 1:
        step(0, 0)
    else:
        lax.fori_loop(0, trips, step, 0)


def group_total(entries):
    lane = lax.broadcasted_iota(jnp.int32, entries.shape, 1)
    for bit in (1, 2):
        up = pltpu.roll(entries, C - bit, 1)
        down = pltpu.roll(entries, bit, 1)
        entries = entries + jnp.where((lane & bit) == 0, up, down)
    return entries


def pick_columns(entries, picks):
    count = entries.shape[0]
    parts = []
    for _ in range(3):
        parts.append(entries.astype(bf16))
        entries = entries - parts[-1].astype(f32)
    picked = jnp.dot(
        jnp.concatenate(parts, axis=0), picks.astype(bf16), preferred_element_type=f32
    )
    return picked[0:count] + picked[count : 2 * count] + picked[2 * count :]


INNER = ROWS * (COLS - 2)


def hidden_kernel(
    valid_ref, order_ref, lead_ref, arrived_ref, near, far, hidden_ref, means_ref, spreads_ref,
    wide, taps, carry,
):
    conv_setup(taps, carry)
    none = jnp.zeros((CHUNK * ROWS, C), f32)
    for u in range(UNROLL):
        put_column(wide.at[u], 7, none)
        put_column(wide.at[u], 8 + COLS, none)
    means_ref[...] = jnp.zeros_like(means_ref)
    spreads_ref[...] = jnp.zeros_like(spreads_ref)
    column = lax.broadcasted_iota(jnp.int32, (POS, C), 0) % COLS
    inner = (column > 0) & (column < COLS - 1)

    def chunk_step(u, start, count, block_of):
        for k in range(count // 2):
            block = block_of(k).astype(f32)
            for row in range(2 * ROWS):
                at = (k * 2 * ROWS + row) * PITCH + 8
                wide[u, at : at + COLS] = block[row * COLS : (row + 1) * COLS]
        totals = conv_chunk(valid_ref, start, count, wide.at[u], taps.at[u], near, far, carry)
        for q in range(count):
            frame = start + q
            own = totals[q]
            hidden_ref[frame] = own
            mean = jnp.sum(jnp.where(inner, own, 0.0), axis=0, keepdims=True) / INNER
            centred = jnp.where(inner, own - mean, 0.0)
            means_ref[pl.ds(frame, 1), :] = mean
            spreads_ref[pl.ds(frame, 1), :] = jnp.sum(centred * centred, axis=0, keepdims=True)

    def own_block(at):
        return lambda k: block_at(arrived_ref, order_ref[0, at // 2 + k])

    chunk_step(UNROLL - 1, 0, LEAD, lambda k: lead_ref[k * 2 * POS : (k + 1) * 2 * POS])
    over_chunks(lambda u, at: chunk_step(u, LEAD + at, CHUNK, own_block(at)))


def first_layer(valid, order, lead, arrived, near, far):
    length = LEAD + 2 * OWN
    sums = jax.ShapeDtypeStruct((2 * HALF, C), f32)
    return pl.pallas_call(
        hidden_kernel,
        out_shape=(jax.ShapeDtypeStruct((length, POS, C), f32), sums, sums),
        in_specs=[smem()] * 2 + [vmem()] * 4,
        out_specs=(vmem(),) * 3,
        scratch_shapes=conv_scratch(),
        compiler_params=params(24),
        cost_estimate=pl.CostEstimate(
            flops=2 * length * POS * 27 * C * C, bytes_accessed=4 * MIB, transcendentals=0
        ),
        name="first_layer",
    )(valid, order, lead, arrived, near, far)


def edge_kernel(
    valid_ref, own_l, own_r, halo_l, halo_r, joined, means_ref, spreads_ref,
    edges_ref, stats_ref, means, spreads,
):
    row = lax.broadcasted_iota(jnp.int32, (EDGE_ROWS, C), 0) % ROWS
    length = EDGE_ROWS // ROWS

    def rows_of(ref, c):
        column = ref[c * EDGE_ROWS : (c + 1) * EDGE_ROWS].astype(f32)
        above = jnp.where(row == 0, 0.0, pltpu.roll(column, 1, 0))
        below = jnp.where(row == ROWS - 1, 0.0, pltpu.roll(column, EDGE_ROWS - 1, 0))
        return [piece.astype(bf16) for piece in (above, column, below)]

    for side, refs in enumerate(((halo_l, own_l), (own_r, halo_r))):
        columns = [rows_of(ref, c) for ref in refs for c in range(2)]
        for k in range(2):
            windows = jnp.concatenate(sum(columns[k : k + 3], []), axis=1)
            product = jnp.dot(windows, joined[...], preferred_element_type=f32)

            def part(frame, lag):
                rows = slice(frame * ROWS, (frame + 1) * ROWS)
                return product[rows, lag * C : (lag + 1) * C]

            at = 2 * side + k
            edges_ref[at, 0 : 2 * ROWS] = jnp.zeros((2 * ROWS, C), f32)
            for frame in range(2, length):
                edges_ref[at, frame * ROWS : (frame + 1) * ROWS] = (
                    part(frame, 0)
                    + valid_ref[0, frame] * part(frame - 1, 1)
                    + valid_ref[1, frame] * part(frame - 2, 2)
                )

    means[...] = jnp.zeros_like(means)
    spreads[...] = jnp.zeros_like(spreads)
    outer = [edges_ref[at].reshape(length, ROWS, C) for at in (1, 2)]
    mean = jnp.sum(outer[0] + outer[1], axis=1, keepdims=True) / (2 * ROWS)
    apart = [(entries - mean) * (entries - mean) for entries in outer]
    means[0:length] = mean.reshape(length, C)
    spreads[0:length] = jnp.sum(apart[0] + apart[1], axis=1)
    off = means[...] - means_ref[...]
    local = means_ref[...] + off * (2 * ROWS / POS)
    spread = spreads_ref[...] + spreads[...] + off * off * (INNER * 2 * ROWS / POS)

    mean = group_total(local) / 4
    off = local - mean
    spread = group_total(spread + POS * off * off)
    pieces = (mean[:HALF], spread[:HALF], mean[HALF:], spread[HALF:])
    channel = lax.broadcasted_iota(jnp.int32, (4 * C, C), 0)
    lane = lax.broadcasted_iota(jnp.int32, (4 * C, C), 1)
    picks = channel == C * (lane // GROUPS) + (C // GROUPS) * (lane % GROUPS)
    packed = pick_columns(jnp.concatenate(pieces, axis=1), picks.astype(f32))
    for peer in range(stats_ref.shape[0]):
        stats_ref[peer] = packed


def finish_hidden(valid, own_l, own_r, halo_l, halo_r, joined, means, spreads, tiles):
    return pl.pallas_call(
        edge_kernel,
        out_shape=(
            jax.ShapeDtypeStruct((4, EDGE_ROWS, C), f32),
            jax.ShapeDtypeStruct((tiles, HALF, C), f32),
        ),
        in_specs=[smem()] + [vmem()] * 7,
        out_specs=(vmem(),) * 2,
        scratch_shapes=[pltpu.VMEM((2 * HALF, C), f32), pltpu.VMEM((2 * HALF, C), f32)],
        compiler_params=params(),
        name="finish_hidden",
    )(valid, own_l, own_r, halo_l, halo_r, joined, means, spreads)


def combine_stats(stats_ref, gain_ref, means, scales):
    tiles = stats_ref.shape[0]
    here = POS * (C // GROUPS)
    lane = lax.broadcasted_iota(jnp.int32, (HALF, C), 1)
    is_mean = (lane // GROUPS) % 2 == 0
    total = stats_ref[0]
    for peer in range(1, tiles):
        total = total + stats_ref[peer]
    mean = total / tiles
    apart = jnp.zeros((HALF, C), f32)
    for peer in range(tiles):
        off = stats_ref[peer] - mean
        apart = apart + off * off
    apart = jnp.where(is_mean, apart, 0.0)
    variance = (total + here * pltpu.roll(apart, GROUPS, 1)) / (here * tiles)
    packed = jnp.where(is_mean, mean, lax.rsqrt(jnp.where(is_mean, 1.0, variance) + EPSILON))
    source = lax.broadcasted_iota(jnp.int32, (C, 4 * C), 0)
    column = lax.broadcasted_iota(jnp.int32, (C, 4 * C), 1)
    picks = source == GROUPS * (column // C) + (column % C) // (C // GROUPS)
    spread_out = pick_columns(packed, picks.astype(f32))
    means[0:HALF] = spread_out[:, 0:C]
    scales[0:HALF] = spread_out[:, C : 2 * C]
    means[HALF:] = spread_out[:, 2 * C : 3 * C]
    scales[HALF:] = spread_out[:, 3 * C :]
    scales[...] = scales[...] * gain_ref[...]


def silu(v):
    return v * (1.0 / (1.0 + jnp.exp(-v)))


def output_kernel(
    valid_ref, order_ref, hidden_ref, edges_ref, stats_ref, arrived_ref,
    gain_ref, norm_bias_ref, near, far, bias_ref, out_ref,
    wide, taps, carry, means, scales, halo, staged, sems,
):
    conv_setup(taps, carry)
    combine_stats(stats_ref, gain_ref, means, scales)
    has_left = valid_ref[2, 0]
    has_right = valid_ref[2, 1]

    def norm(hidden, frame):
        centred = hidden - means[pl.ds(frame, 1), :]
        return silu(centred * scales[pl.ds(frame, 1), :] + norm_bias_ref[...])

    def chunk_step(u, start, count):
        for q in range(count):
            frame = start + q
            active = norm(hidden_ref[frame], frame)
            for r in range(ROWS):
                at = (q * ROWS + r) * PITCH + 8
                wide[u, at : at + COLS] = active[r * COLS : (r + 1) * COLS]
            at = pl.ds(pl.multiple_of(frame * ROWS, ROWS), ROWS)
            for k, inside in enumerate((has_left, 1.0, 1.0, has_right)):
                halo[u, k, q * ROWS : (q + 1) * ROWS] = norm(edges_ref[k, at], frame) * inside
        for k, column in enumerate((7, 8, 7 + COLS, 8 + COLS)):
            put_column(wide.at[u], column, halo[u, k, 0 : count * ROWS])
        return conv_chunk(valid_ref, start, count, wide.at[u], taps.at[u], near, far, carry)

    def own_chunk(u, start):
        totals = chunk_step(u, LEAD + start, CHUNK)
        for k in range(CHUNK // 2):
            block = block_at(arrived_ref, order_ref[0, start // 2 + k]).astype(f32)
            total = block + (jnp.concatenate(totals[2 * k : 2 * k + 2], axis=0) + bias_ref[...])
            rows = pl.ds(pl.multiple_of((start + 2 * k) * POS, 2 * POS), 2 * POS)
            staged[rows] = total.astype(bf16)
        copy_out(start).start()

    def copy_out(start):
        rows = pl.ds(pl.multiple_of(start * POS, CHUNK * POS), CHUNK * POS)
        sem = sems.at[lax.div(jnp.int32(start), jnp.int32(CHUNK))]
        return pltpu.make_async_copy(staged.at[rows], out_ref.at[rows], sem)

    chunk_step(UNROLL - 1, LEAD - 2, 2)
    over_chunks(own_chunk)
    for start in range(0, 2 * OWN, CHUNK):
        copy_out(start).wait()


def second_layer(valid, order, hidden, edges, stats, arrived, gain, norm_bias, near, far, bias):
    return pl.pallas_call(
        output_kernel,
        out_shape=jax.ShapeDtypeStruct((2 * OWN * POS, C), bf16),
        in_specs=[smem()] * 2 + [vmem()] * 9,
        out_specs=hbm_only(),
        scratch_shapes=conv_scratch()
        + [
            pltpu.VMEM((2 * HALF, C), f32),
            pltpu.VMEM((2 * HALF, C), f32),
            pltpu.VMEM((UNROLL, 4, CHUNK * ROWS, C), f32),
            pltpu.VMEM((2 * OWN * POS, C), bf16),
            pltpu.SemaphoreType.DMA((2 * OWN // CHUNK,)),
        ],
        compiler_params=params(24),
        name="second_layer",
    )(valid, order, hidden, edges, stats, arrived, gain, norm_bias, near, far, bias)


def lag_masks(clip_frames, first_frame, length):
    clip_ends = jnp.cumsum(clip_frames)

    def clip_of(frames):
        ids = jnp.sum((frames[:, None] >= clip_ends[None, :]).astype(jnp.int32), axis=1)
        return jnp.where(frames < 0, -1, ids)

    frames = first_frame + jnp.arange(length, dtype=jnp.int32)
    here = clip_of(frames)
    return jnp.stack([clip_of(frames - lag) == here for lag in (1, 2)])


def swap_edges(left, right):
    count = lax.axis_size("tile")
    from_left = lax.ppermute(right, "tile", [(i, i + 1) for i in range(count - 1)])
    from_right = lax.ppermute(left, "tile", [(i + 1, i) for i in range(count - 1)])
    return from_left, from_right


def shards(
    video, slot_block, clip_frames, conv1_weight, norm_gain, norm_bias, conv2_weight, conv2_bias
):
    owners = lax.axis_size("tm")
    tiles = lax.axis_size("tile")
    position = lax.axis_index("tm")
    tile = lax.axis_index("tile")
    length = 2 * OWN

    outgoing = send_blocks(slot_block, video, owners)
    arrived = lax.all_to_all(outgoing, "tm", split_axis=0, concat_axis=0, tiled=True)

    inside = jnp.stack([tile > 0, tile < tiles - 1] + [tile < 0] * (length + LEAD - 2))
    valid = jnp.concatenate(
        [lag_masks(clip_frames, position * length - LEAD, length + LEAD), inside[None]]
    ).astype(f32)

    weight_edge, near1, far1, near2, far2, token = join_weights(conv1_weight, conv2_weight)
    order, tail = block_order(arrived, (valid, token))
    lead = lax.ppermute(tail, "tm", [(i, i + 1) for i in range(owners - 1)])
    left, right = own_edges(order, arrived)
    left, right = lead_edges(lead, left, right)
    from_left, from_right = swap_edges(left, right)
    hidden, means, spreads = first_layer(valid, order, lead, arrived, near1, far1)
    edges, stats = finish_hidden(
        valid, left, right, from_left, from_right, weight_edge, means, spreads, tiles
    )
    stats = lax.all_to_all(stats, "tile", split_axis=0, concat_axis=0, tiled=True)
    encoded = second_layer(
        valid, order, hidden, edges, stats, arrived, norm_gain[None], norm_bias[None],
        near2, far2, conv2_bias[None],
    )
    return encoded.reshape((length,) + video.shape[2:])


def solution(mesh):
    placed = (P("tm", None, None, "tile", None), P("tm"), P(), P(), P(), P(), P(), P())
    return jax.shard_map(
        shards, mesh=mesh, in_specs=placed, out_specs=P("tm", None, "tile", None), check_vma=False
    )
```
